128 devices in a mesh: seq: 32 (over z, y, core), batch: 4 (over x).
Axes of the slice: x: 4, y: 4, z: 4, core: 2. Of those that a mesh axis runs over, the one named last changes fastest.
Arguments:
- queries: bfloat16 [65536, 2048], P(('batch', 'seq')), parts along dimension 0, may hold values from -6 to 6
- keys: bfloat16 [65536, 2048], P(('batch', 'seq')), parts along dimension 0, may hold values from -0.5 to 0.5
- values: bfloat16 [65536, 2048], P(('batch', 'seq')), parts along dimension 0, may hold values from -6 to 6
- log_gate: float32 [65536, 2048], P(('batch', 'seq')), parts along dimension 0, may hold values from -1 to 0, as said below
Outputs:
- attended: bfloat16 [65536, 2048], P(('batch', 'seq')), parts along dimension 0
The draws below stay inside these ranges and needn't reach their ends.
There are 4 independent parts, one for each index of `batch`. The reference program is written for one: setup_inputs(seed, part) draws one part's arguments, and reference() takes and returns one part's arrays. A program takes and returns all parts, laid end to end along the dimension named above; each array names one. Nothing has to cross between parts.
Inputs may be any that keep to these rules, and one draw needn't show every extreme that they name: `log_gate`: log-decays of the forget gate per token and key channel; within each aligned block of 128 tokens the log-decays of one key channel sum to at least -40.
All inputs are finite; a program needn't handle non-finite values.
Results may differ from the reference program's by a relative error of at most 0.0063.
Values sent between devices are 32-bit elements; how exact they have to be, the bound alone decides.
No kernel may reach another device: no remote copies, remote signals or barrier semaphores. Data moves between devices by JAX's collectives and lax.ppermute only.
A program may use at most 128 MiB of HBM per device.

```python
import math
import jax
import jax.numpy as jnp
from jax import lax

H = 16
DK = 128
DV = 128
GROUP = 128
TEXT_SPAN = 16384
KEY_CHANNELS = 2048


def draw_log_gate(key, part):
    key = jax.random.fold_in(key, 11)
    segment_transfers = jax.random.split(key, 6)
    lasting_share = 0.5
    jitter_low = 0.5
    jitter_high = 1.5
    lasting = jax.random.uniform(segment_transfers[0], (KEY_CHANNELS,)) < lasting_share
    fast_speed = jnp.exp(jax.random.uniform(segment_transfers[1], (KEY_CHANNELS,), minval=math.log(1.0 / 50.0), maxval=math.log(1.0 / 30.0)))
    speeds = jnp.where(lasting, 0.4 / TEXT_SPAN, fast_speed)
    jitter = jax.random.uniform(segment_transfers[2], (TEXT_SPAN, KEY_CHANNELS), minval=jitter_low, maxval=jitter_high)
    multiplier_grid = jnp.exp(jax.random.uniform(segment_transfers[3], (TEXT_SPAN // GROUP, KEY_CHANNELS), minval=math.log(0.5), maxval=math.log(2.0)))
    block_factor = jnp.repeat(multiplier_grid, GROUP, axis=0)
    third_extent = TEXT_SPAN // 3
    transfer_starts = jax.random.randint(segment_transfers[4], (3, KEY_CHANNELS), 0, third_extent)
    transfer_targets = transfer_starts + (jnp.arange(3) * third_extent)[:, None]
    transfer_sizes = jax.random.uniform(segment_transfers[5], (3, KEY_CHANNELS), minval=0.22, maxval=0.69)
    segment_locations = jnp.arange(TEXT_SPAN)[:, None]
    discard_region = jnp.zeros((TEXT_SPAN, KEY_CHANNELS), jnp.float32)
    for transfer_total in range(3):
        discard_region = discard_region + jnp.where(segment_locations == transfer_targets[transfer_total][None, :], transfer_sizes[transfer_total][None, :], 0.0)
    return (-(speeds[None, :] * jitter * block_factor) - discard_region).astype(jnp.float32)


def block_levels(own_key, extent, shards, least, largest):
    gain, own = 1.0, jax.random.fold_in(own_key, 6)
    for axis_at, parts in shards:
        heights = jnp.exp(jax.random.uniform(jax.random.fold_in(own, axis_at), (parts,), jnp.float32, least / len(shards), largest / len(shards)))
        gain = gain * jnp.repeat(heights, extent[axis_at] // parts).reshape([-1 if axis == axis_at else 1 for axis in range(len(extent))])
    return gain


def gaussian(key, shape, width, limit, shards=(), dtype=jnp.bfloat16):
    result = width * jax.random.normal(key, shape, jnp.float32)
    if shards:
        result = result * block_levels(key, shape, shards, -0.22, 0.18)
    return jnp.clip(result, -limit, limit).astype(dtype)


def setup_inputs(seed: int = 0, part: int = 0) -> dict:
    splits = jax.random.split(jax.random.key(seed), 5)
    part_splits = jax.random.split(jax.random.fold_in(splits[4], part), 5)
    queries = gaussian(part_splits[0], (TEXT_SPAN, H * DK), 1.0, 6.0, ((0, 32),))
    keys = gaussian(part_splits[1], (TEXT_SPAN, H * DK), (4 * TEXT_SPAN ** -0.5), 0.5, ((0, 32),))
    values = gaussian(part_splits[2], (TEXT_SPAN, H * DV), 1.0, 6.0, ((0, 32),))
    log_gate = draw_log_gate(jax.random.fold_in(jax.random.fold_in(splits[4], part), 71), part)
    return dict(queries=queries, keys=keys, values=values, log_gate=log_gate)


def rounded(value):
    return lax.optimization_barrier(value.astype(jnp.bfloat16)).astype(jnp.float32)


def reference(queries, keys, values, log_gate):
    groups = TEXT_SPAN // GROUP
    query_blocks = queries.reshape(groups, GROUP, H, DK)
    key_blocks = keys.reshape(groups, GROUP, H, DK)
    value_blocks = values.reshape(groups, GROUP, H, DV)
    gate_blocks = log_gate.reshape(groups, GROUP, H, DK)
    causal = jnp.arange(GROUP)[:, None] >= jnp.arange(GROUP)[None, :]

    def advance_group(carried, inputs):
        local_query, key_here, value_here, gate_here = inputs
        cumulative = jnp.cumsum(gate_here, axis=0)
        totals = cumulative[-1]
        query_scaled = rounded(local_query.astype(jnp.float32) * (DK ** -0.5) * jnp.exp(cumulative))
        key_inverse = rounded(key_here.astype(jnp.float32) * jnp.exp(-cumulative))
        key_to_end = rounded(key_here.astype(jnp.float32) * jnp.exp(totals[None] - cumulative))
        value_float = value_here.astype(jnp.float32)
        scores = jnp.einsum("thc,shc->hts", query_scaled, key_inverse)
        scores = rounded(jnp.where(causal[None], scores, 0.0))
        within = jnp.einsum("hts,shv->thv", scores, value_float)
        across = jnp.einsum("thc,hcv->thv", query_scaled, rounded(carried))
        attention_result = (within + across).astype(jnp.bfloat16)
        updated = jnp.exp(totals)[..., None] * carried + jnp.einsum("shc,shv->hcv", key_to_end, value_float)
        return updated, attention_result

    initial = jnp.zeros((H, DK, DV), jnp.float32)
    final_state, outputs = lax.scan(advance_group, initial, (query_blocks, key_blocks, value_blocks, gate_blocks))
    return outputs.reshape(TEXT_SPAN, H * DV)
```

```python
import functools
import math

import jax
import jax.numpy as jnp
from jax import lax
from jax.experimental import pallas as pl
from jax.experimental.pallas import tpu as pltpu
from jax.sharding import PartitionSpec as P

H = 16
DK = 128
DV = 128
GROUP = 128
HALF = H // 2
WIDTH = HALF * DK
HEADS_STEP = 2
LANES = HEADS_STEP * DK
STEPS = HALF // HEADS_STEP
EARLY = 2
CHUNKS = 4
ROWS = 64
SLICE = ROWS + 8
LOG2E = math.log2(math.e)
LOG2_SCALE = -0.5 * math.log2(DK)

NT = (((1,), (1,)), ((), ()))
TN = (((0,), (0,)), ((), ()))

VMEM = pl.BlockSpec(memory_space=pltpu.VMEM)
SMEM = pl.BlockSpec(memory_space=pltpu.SMEM)
HBM = pl.BlockSpec(memory_space=pltpu.HBM)
ANY = pl.BlockSpec(memory_space=pl.ANY)


def in_vmem(x):
    return pltpu.with_memory_space_constraint(x, pltpu.VMEM)


def in_hbm(x):
    return pltpu.with_memory_space_constraint(x, pltpu.HBM)


def dot(a, b, dims=(((1,), (0,)), ((), ()))):
    return lax.dot_general(a, b, dims, preferred_element_type=jnp.float32)


def triangle(strict_upper):
    row = lax.broadcasted_iota(jnp.int32, (GROUP, 2 * GROUP), 0)
    col = lax.broadcasted_iota(jnp.int32, (GROUP, 2 * GROUP), 1)
    col = jnp.where(col >= GROUP, col - GROUP, col)
    keep = col > row if strict_upper else col <= row
    return jnp.where(keep, 1.0, 0.0).astype(jnp.bfloat16)


def partial_sums(ones, gate):
    high = gate.astype(jnp.bfloat16)
    low = (gate - high.astype(jnp.float32)).astype(jnp.bfloat16)
    return dot(ones, jnp.concatenate([high, low], axis=0))


def columns(half, step):
    return pl.ds(pl.multiple_of(half * WIDTH + step * LANES, LANES), LANES)


def states_step(step, gate_ref, key_ref, value_ref, out_ref):
    ones = triangle(True)
    state = [jnp.zeros((DV, DK), jnp.float32)] * HEADS_STEP
    total = [jnp.zeros((1, DK), jnp.float32)] * HEADS_STEP
    cols = pl.ds(step * LANES, LANES)
    for group in range(gate_ref.shape[0] // GROUP):
        rows = pl.ds(group * GROUP, GROUP)
        gate = gate_ref[rows, cols] * LOG2E
        later = partial_sums(ones, gate)
        gamma = later[0:1] + gate[0:1]
        to_end = (key_ref[rows, cols].astype(jnp.float32) * jnp.exp2(later)).astype(jnp.bfloat16)
        decay = jnp.exp2(gamma)
        for head in range(HEADS_STEP):
            at = slice(head * DK, (head + 1) * DK)
            value = value_ref[rows, pl.ds(step * LANES + head * DV, DV)]
            state[head] = state[head] * decay[:, at] + dot(value, to_end[:, at], TN)
            total[head] = total[head] + gamma[:, at]
    for head in range(HEADS_STEP):
        for part in range(2):
            at = 2 * (step * HEADS_STEP + head) + part
            out_ref[at, 0:ROWS, :] = state[head][ROWS * part : ROWS * (part + 1)]
            out_ref[at, ROWS:SLICE, :] = jnp.broadcast_to(total[head], (SLICE - ROWS, DK))


def column_copies(half, steps, sources, targets, sems):
    copies = []
    for step in steps:
        for source, target in zip(sources, targets):
            at = pl.ds(step * LANES, LANES)
            copies.append(
                pltpu.make_async_copy(source.at[:, columns(half, step)], target.at[:, at], sems.at[len(copies)])
            )
    for copy in copies:
        copy.start()
    return [copies[i : i + len(sources)] for i in range(0, len(copies), len(sources))]


def wait_all(copies):
    for copy in copies:
        copy.wait()


def rest_states_kernel(
    core_ref, gate_hbm, key_hbm, value_hbm, out_ref, own_gate, own_key, own_value, gate, key, value, sems, own_sems
):
    sources = (gate_hbm, key_hbm, value_hbm)
    mine = column_copies(1 - core_ref[0], range(STEPS), sources, (gate, key, value), sems)
    early = column_copies(core_ref[0], range(EARLY), sources, (own_gate, own_key, own_value), own_sems)
    for step in range(STEPS):
        wait_all(mine[step])
        states_step(step, gate, key, value, out_ref)
    for copies in early:
        wait_all(copies)


def rest_states(core, gate, keys, values):
    tokens = keys.shape[0]
    kinds = [x.dtype for x in (gate, keys, values)]
    return pl.pallas_call(
        rest_states_kernel,
        in_specs=[SMEM, HBM, HBM, HBM],
        out_specs=[VMEM] * 4,
        out_shape=[pltpu.VMEM((2 * HALF, SLICE, DK), jnp.float32)]
        + [pltpu.VMEM((tokens, EARLY * LANES), kind) for kind in kinds],
        scratch_shapes=[pltpu.VMEM((tokens, WIDTH), kind) for kind in kinds]
        + [pltpu.SemaphoreType.DMA((3 * STEPS,)), pltpu.SemaphoreType.DMA((3 * EARLY,))],
        compiler_params=pltpu.CompilerParams(vmem_limit_bytes=8 << 20),
        cost_estimate=pl.CostEstimate(flops=10**9, bytes_accessed=9 * 10**6, transcendentals=10**6),
        name="rest_states",
    )(core, in_hbm(gate), in_hbm(keys), in_hbm(values))


def own_states_kernel(
    core_ref, gate_hbm, key_hbm, value_hbm, early_gate, early_key, early_value, out_ref, gate, key, value, sems
):
    mine = column_copies(
        core_ref[0], range(EARLY, STEPS), (gate_hbm, key_hbm, value_hbm), (gate, key, value), sems
    )
    for step in range(EARLY):
        states_step(step, early_gate, early_key, early_value, out_ref)
    for step in range(EARLY, STEPS):
        wait_all(mine[step - EARLY])
        states_step(step, gate, key, value, out_ref)


def own_states(core, gate, keys, values, early):
    tokens = keys.shape[0]
    kinds = [x.dtype for x in (gate, keys, values)]
    return pl.pallas_call(
        own_states_kernel,
        in_specs=[SMEM, HBM, HBM, HBM] + [VMEM] * 3,
        out_specs=VMEM,
        out_shape=pltpu.VMEM((2 * HALF, SLICE, DK), jnp.float32),
        scratch_shapes=[pltpu.VMEM((tokens, WIDTH), kind) for kind in kinds]
        + [pltpu.SemaphoreType.DMA((3 * (STEPS - EARLY),))],
        compiler_params=pltpu.CompilerParams(vmem_limit_bytes=8 << 20),
        cost_estimate=pl.CostEstimate(flops=10**9, bytes_accessed=5 * 10**6, transcendentals=10**6),
        name="own_states",
    )(core, in_hbm(gate), in_hbm(keys), in_hbm(values), *map(in_vmem, early))


def combine_kernel(core_ref, mine_ref, other_ref, out_hbm, other_hbm, out_ref, sems):
    copies = [pltpu.make_async_copy(other_ref, other_hbm, sems.at[CHUNKS])]
    copies[0].start()
    first = core_ref[0] == 0
    length = mine_ref.shape[0] // CHUNKS
    for chunk in range(CHUNKS):
        at = pl.ds(chunk * length, length)
        mine_total = mine_ref[at, ROWS:SLICE, :]
        other_total = other_ref[at, ROWS:SLICE, :]
        mine_weight = jnp.where(first, jnp.exp2(other_total), 1.0)[:, 0:1]
        other_weight = jnp.where(first, 1.0, jnp.exp2(mine_total))[:, 0:1]
        out_ref[at, 0:ROWS, :] = mine_ref[at, 0:ROWS, :] * mine_weight + other_ref[at, 0:ROWS, :] * other_weight
        out_ref[at, ROWS:SLICE, :] = mine_total + other_total
        copies.append(pltpu.make_async_copy(out_ref.at[at], out_hbm.at[at], sems.at[chunk]))
        copies[-1].start()
    wait_all(copies)


def combine(core, mine, other):
    return pl.pallas_call(
        combine_kernel,
        in_specs=[SMEM, VMEM, VMEM],
        out_specs=[HBM, HBM],
        out_shape=[pltpu.HBM(mine.shape, jnp.float32)] * 2,
        scratch_shapes=[pltpu.VMEM(mine.shape, jnp.float32), pltpu.SemaphoreType.DMA((CHUNKS + 1,))],
        compiler_params=pltpu.CompilerParams(vmem_limit_bytes=4 << 20),
        name="combine",
    )(core, in_vmem(mine), in_vmem(other))


def prefix_kernel(in_ref, _, out_hbm, out_ref, sems):
    running = jnp.zeros((ROWS, DK), jnp.float32)
    chips = in_ref.shape[0]
    copies = []
    for chip in range(chips):
        out_ref[chip] = running
        if (chip + 1) % CHUNKS == 0:
            at = pl.ds(chip + 1 - CHUNKS, CHUNKS)
            copies.append(pltpu.make_async_copy(out_ref.at[at], out_hbm.at[at], sems.at[len(copies)]))
            copies[-1].start()
        if chip < chips - 1:
            decay = jnp.exp2(in_ref[chip, ROWS : ROWS + 1, :])
            running = running * decay + in_ref[chip, 0:ROWS, :]
    wait_all(copies)


def prefix(received, after):
    shape = (received.shape[0], ROWS, DK)
    return pl.pallas_call(
        prefix_kernel,
        in_specs=[VMEM, ANY],
        out_specs=HBM,
        out_shape=pltpu.HBM(shape, jnp.float32),
        scratch_shapes=[pltpu.VMEM(shape, jnp.float32), pltpu.SemaphoreType.DMA((shape[0] // CHUNKS,))],
        compiler_params=pltpu.CompilerParams(vmem_limit_bytes=4 << 20),
        name="prefix",
    )(in_vmem(received), after)


def local_step(step, second, query_ref, key_ref, value_ref, gate_ref, init_ref, local_ref, decayed_ref):
    ones = triangle(False)
    row = lax.broadcasted_iota(jnp.int32, (GROUP, GROUP), 0)
    col = lax.broadcasted_iota(jnp.int32, (GROUP, GROUP), 1)
    causal = row >= col
    cols = pl.ds(step * LANES, LANES)
    state, total = [], []
    for head in range(HEADS_STEP):
        at = 2 * (step * HEADS_STEP + head)
        start = jnp.concatenate([init_ref[at, 0:ROWS, :], init_ref[at + 1, 0:ROWS, :]], axis=0)
        state.append(jnp.where(second, start, 0.0))
        total.append(jnp.where(second, init_ref[at, ROWS : ROWS + 1, :], 0.0))
    groups = gate_ref.shape[0] // GROUP
    for group in range(groups):
        rows = pl.ds(group * GROUP, GROUP)
        inclusive = partial_sums(ones, gate_ref[rows, cols] * LOG2E)
        gamma = inclusive[GROUP - 1 : GROUP]
        decay = jnp.exp2(gamma)
        query = query_ref[rows, cols].astype(jnp.float32) * jnp.exp2(inclusive + LOG2_SCALE)
        key = key_ref[rows, cols].astype(jnp.float32) * jnp.exp2(-inclusive)
        query_scaled = query.astype(jnp.bfloat16)
        key_inverse = key.astype(jnp.bfloat16)
        to_end = (key * decay).astype(jnp.bfloat16)
        before = jnp.exp2(jnp.concatenate(total, axis=1))
        decayed_ref[rows, cols] = (query * before).astype(jnp.bfloat16)
        for head in range(HEADS_STEP):
            at = slice(head * DK, (head + 1) * DK)
            head_cols = pl.ds(step * LANES + head * DV, DV)
            value = value_ref[rows, head_cols]
            scores = dot(query_scaled[:, at], key_inverse[:, at], NT)
            scores = jnp.where(causal, scores, 0.0).astype(jnp.bfloat16)
            out = dot(scores, value) + dot(query_scaled[:, at], state[head].astype(jnp.bfloat16), NT)
            local_ref[rows, head_cols] = out.astype(local_ref.dtype)
            if group < groups - 1:
                state[head] = state[head] * decay[:, at] + dot(value, to_end[:, at], TN)
                total[head] = total[head] + gamma[:, at]


def local_kernel(rest, core_ref, query_hbm, key_hbm, value_hbm, gate_hbm, init_any, local_out, decayed_out, done_ref, *refs):
    query, key, value, gate, init, sems, init_sem = refs[:7]
    core = core_ref[0]
    half = 1 - core if rest else core
    fetch = pltpu.make_async_copy(init_any, init, init_sem)
    fetch.start()
    copies = column_copies(
        half, range(STEPS), (gate_hbm, query_hbm, key_hbm, value_hbm), (gate, query, key, value), sems
    )
    fetch.wait()
    local_ref, decayed_ref = refs[7:9] if rest else (local_out, decayed_out)
    stores = []
    for step in range(STEPS):
        wait_all(copies[step])
        local_step(step, core == 1, query, key, value, gate, init, local_ref, decayed_ref)
        if rest:
            at = pl.ds(step * LANES, LANES)
            for ref, out in ((local_ref, local_out), (decayed_ref, decayed_out)):
                stores.append(pltpu.make_async_copy(ref.at[:, at], out.at[:, at], refs[9].at[len(stores)]))
                stores[-1].start()
    wait_all(stores)
    done_ref[...] = jnp.zeros_like(done_ref)


def local_part(rest, core, queries, keys, values, gate, init):
    tokens = keys.shape[0]
    place = pltpu.HBM if rest else pltpu.VMEM
    half = ((tokens, WIDTH), jnp.bfloat16)
    scratch = [pltpu.VMEM((tokens, WIDTH), x.dtype) for x in (queries, keys, values, gate)]
    scratch += [pltpu.VMEM(init.shape, init.dtype), pltpu.SemaphoreType.DMA((4 * STEPS,)), pltpu.SemaphoreType.DMA]
    if rest:
        scratch += [pltpu.VMEM(*half)] * 2 + [pltpu.SemaphoreType.DMA((2 * STEPS,))]
    return pl.pallas_call(
        functools.partial(local_kernel, rest),
        in_specs=[SMEM] + [HBM] * 5,
        out_specs=[HBM if rest else VMEM] * 2 + [VMEM],
        out_shape=[place(*half)] * 2 + [jax.ShapeDtypeStruct((8, DK), jnp.float32)],
        scratch_shapes=scratch,
        compiler_params=pltpu.CompilerParams(vmem_limit_bytes=12 << 20),
        cost_estimate=pl.CostEstimate(flops=4 * 10**9, bytes_accessed=8 * 10**6, transcendentals=10**6),
        name="rest_local" if rest else "own_local",
    )(core, in_hbm(queries), in_hbm(keys), in_hbm(values), in_hbm(gate), in_hbm(init))


def final_step(step, local_ref, decayed_ref, entry_ref, out_ref):
    for head in range(step * HEADS_STEP, (step + 1) * HEADS_STEP):
        at = slice(head * DK, (head + 1) * DK)
        across = dot(decayed_ref[:, at], entry_ref[at, :].astype(jnp.bfloat16), NT)
        out_ref[:, at] = (local_ref[:, at].astype(jnp.float32) + across).astype(jnp.bfloat16)


def final_steps(half, local_ref, decayed_ref, entry_ref, out_hbm, out_ref, sems):
    copies = []
    for step in range(STEPS):
        final_step(step, local_ref, decayed_ref, entry_ref, out_ref)
        at = pl.ds(step * LANES, LANES)
        copies.append(pltpu.make_async_copy(out_ref.at[:, at], out_hbm.at[:, columns(half, step)], sems.at[step]))
        copies[-1].start()
    wait_all(copies)


def own_final_kernel(core_ref, local, decayed, entry, local_hbm, decayed_hbm, _, out_hbm, rest_local, rest_decayed, *refs):
    out_ref, sems, fetch_sems = refs
    fetches = [
        pltpu.make_async_copy(local_hbm, rest_local, fetch_sems.at[0]),
        pltpu.make_async_copy(decayed_hbm, rest_decayed, fetch_sems.at[1]),
    ]
    for fetch in fetches:
        fetch.start()
    final_steps(core_ref[0], local, decayed, entry, out_hbm, out_ref, sems)
    wait_all(fetches)


def own_final(core, local, decayed, entry, rest_local, rest_decayed, after):
    tokens = local.shape[0]
    return pl.pallas_call(
        own_final_kernel,
        in_specs=[SMEM] + [VMEM] * 3 + [HBM] * 2 + [ANY],
        out_specs=[HBM, VMEM, VMEM],
        out_shape=[jax.ShapeDtypeStruct((tokens, H * DV), jnp.bfloat16)]
        + [pltpu.VMEM(x.shape, x.dtype) for x in (rest_local, rest_decayed)],
        scratch_shapes=[
            pltpu.VMEM((tokens, WIDTH), jnp.bfloat16),
            pltpu.SemaphoreType.DMA((STEPS,)),
            pltpu.SemaphoreType.DMA((2,)),
        ],
        compiler_params=pltpu.CompilerParams(vmem_limit_bytes=8 << 20),
        cost_estimate=pl.CostEstimate(flops=10**9, bytes_accessed=4 * 10**6, transcendentals=0),
        name="own_final",
    )(core, *map(in_vmem, (local, decayed, entry)), in_hbm(rest_local), in_hbm(rest_decayed), after)


def rest_final_kernel(core_ref, local, decayed, entry, _, out_hbm, out_ref, sems):
    final_steps(1 - core_ref[0], local, decayed, entry, out_hbm, out_ref, sems)


def rest_final(core, local, decayed, entry, out):
    tokens = local.shape[0]
    return pl.pallas_call(
        rest_final_kernel,
        in_specs=[SMEM] + [VMEM] * 3 + [ANY],
        out_specs=HBM,
        out_shape=jax.ShapeDtypeStruct((tokens, H * DV), jnp.bfloat16),
        input_output_aliases={4: 0},
        scratch_shapes=[pltpu.VMEM((tokens, WIDTH), jnp.bfloat16), pltpu.SemaphoreType.DMA((STEPS,))],
        compiler_params=pltpu.CompilerParams(vmem_limit_bytes=8 << 20),
        cost_estimate=pl.CostEstimate(flops=10**9, bytes_accessed=4 * 10**6, transcendentals=0),
        name="rest_final",
    )(core, *map(in_vmem, (local, decayed, entry)), out)


def on_device(queries, keys, values, log_gate):
    devices = lax.axis_size("seq")
    chips = devices // 2
    core = lax.rem(lax.axis_index("seq"), 2).astype(jnp.int32)[None]
    swap = [(i, i ^ 1) for i in range(devices)]
    same_core = [[2 * chip + c for chip in range(chips)] for c in range(2)]

    def exchange(blocks):
        return lax.all_to_all(blocks, "seq", split_axis=0, concat_axis=0, axis_index_groups=same_core, tiled=True)

    rest, *early = rest_states(core, log_gate, keys, values)
    own_other = lax.ppermute(rest, "seq", swap)
    own = own_states(core, log_gate, keys, values, early)
    rest_other = lax.ppermute(own, "seq", swap)
    combined, own_other = combine(core, own, own_other)
    received = exchange(combined)
    own_local, own_decayed, own_done = local_part(False, core, queries, keys, values, log_gate, own_other)
    own_entry = exchange(prefix(received, own_done))
    rest_local, rest_decayed, rest_done = local_part(True, core, queries, keys, values, log_gate, rest_other)
    own_entry, rest_done = lax.optimization_barrier((own_entry, rest_done))
    own_entry = own_entry.reshape(HALF * DV, DK)
    rest_entry = lax.ppermute(own_entry, "seq", swap)
    out, local, decayed = own_final(core, own_local, own_decayed, own_entry, rest_local, rest_decayed, rest_done)
    return rest_final(core, local, decayed, rest_entry, out)


def solution(mesh):
    spec = P(("batch", "seq"), None)
    return jax.shard_map(on_device, mesh=mesh, in_specs=(spec,) * 4, out_specs=spec, check_vma=False)
```

```python
import functools
import math

import jax
import jax.numpy as jnp
from jax import lax
from jax.experimental import pallas as pl
from jax.experimental.pallas import tpu as pltpu
from jax.sharding import PartitionSpec as P

H = 16
DK = 128
DV = 128
GROUP = 128
HALF = H // 2
WIDTH = HALF * DK
HEADS_STEP = 2
LANES = HEADS_STEP * DK
STEPS = HALF // HEADS_STEP
EARLY = 2
WIDE = 512
LOCAL_STEPS = WIDTH // WIDE
CHUNKS = 4
ROWS = 64
SLICE = ROWS + 8
LOG2E = math.log2(math.e)
LOG2_SCALE = -0.5 * math.log2(DK)

NT = (((1,), (1,)), ((), ()))
TN = (((0,), (0,)), ((), ()))

VMEM = pl.BlockSpec(memory_space=pltpu.VMEM)
SMEM = pl.BlockSpec(memory_space=pltpu.SMEM)
HBM = pl.BlockSpec(memory_space=pltpu.HBM)
ANY = pl.BlockSpec(memory_space=pl.ANY)


def in_vmem(x):
    return pltpu.with_memory_space_constraint(x, pltpu.VMEM)


def in_hbm(x):
    return pltpu.with_memory_space_constraint(x, pltpu.HBM)


def dot(a, b, dims=(((1,), (0,)), ((), ()))):
    return lax.dot_general(a, b, dims, preferred_element_type=jnp.float32)


def triangle(strict_upper):
    row = lax.broadcasted_iota(jnp.int32, (GROUP, 2 * GROUP), 0)
    col = lax.broadcasted_iota(jnp.int32, (GROUP, 2 * GROUP), 1)
    col = jnp.where(col >= GROUP, col - GROUP, col)
    keep = col > row if strict_upper else col <= row
    return jnp.where(keep, 1.0, 0.0).astype(jnp.bfloat16)


def partial_sums(ones, gate):
    high = gate.astype(jnp.bfloat16)
    low = (gate - high.astype(jnp.float32)).astype(jnp.bfloat16)
    return dot(ones, jnp.concatenate([high, low], axis=0))


def columns(half, step, lanes=LANES):
    return pl.ds(pl.multiple_of(half * WIDTH + step * lanes, lanes), lanes)


def states_step(step, gate_ref, key_ref, value_ref, out_ref):
    ones = triangle(True)
    state = [jnp.zeros((DV, DK), jnp.float32)] * HEADS_STEP
    total = [jnp.zeros((1, DK), jnp.float32)] * HEADS_STEP
    cols = pl.ds(step * LANES, LANES)
    for group in range(gate_ref.shape[0] // GROUP):
        rows = pl.ds(group * GROUP, GROUP)
        gate = gate_ref[rows, cols] * LOG2E
        later = partial_sums(ones, gate)
        gamma = later[0:1] + gate[0:1]
        to_end = (key_ref[rows, cols].astype(jnp.float32) * jnp.exp2(later)).astype(jnp.bfloat16)
        decay = jnp.exp2(gamma)
        for head in range(HEADS_STEP):
            at = slice(head * DK, (head + 1) * DK)
            value = value_ref[rows, pl.ds(step * LANES + head * DV, DV)]
            state[head] = state[head] * decay[:, at] + dot(value, to_end[:, at], TN)
            total[head] = total[head] + gamma[:, at]
    for head in range(HEADS_STEP):
        for part in range(2):
            at = 2 * (step * HEADS_STEP + head) + part
            out_ref[at, 0:ROWS, :] = state[head][ROWS * part : ROWS * (part + 1)]
            out_ref[at, ROWS:SLICE, :] = jnp.broadcast_to(total[head], (SLICE - ROWS, DK))


def column_copies(half, steps, sources, targets, sems, lanes=LANES):
    copies = []
    for step in steps:
        for source, target in zip(sources, targets):
            at = pl.ds(step * lanes, lanes)
            copies.append(
                pltpu.make_async_copy(source.at[:, columns(half, step, lanes)], target.at[:, at], sems.at[len(copies)])
            )
    return [copies[i : i + len(sources)] for i in range(0, len(copies), len(sources))]


def start_all(copies):
    for copy in copies:
        copy.start()


def wait_all(copies):
    for copy in copies:
        copy.wait()


def rest_states_kernel(
    core_ref, gate_hbm, key_hbm, value_hbm, out_ref, own_gate, own_key, own_value, gate, key, value, sems, own_sems
):
    sources = (gate_hbm, key_hbm, value_hbm)
    mine = column_copies(1 - core_ref[0], range(STEPS), sources, (gate, key, value), sems)
    early = column_copies(core_ref[0], range(EARLY), sources, (own_gate, own_key, own_value), own_sems)
    for copies in mine + early:
        start_all(copies)
    for step in range(STEPS):
        wait_all(mine[step])
        states_step(step, gate, key, value, out_ref)
    for copies in early:
        wait_all(copies)


def rest_states(core, gate, keys, values):
    tokens = keys.shape[0]
    kinds = [x.dtype for x in (gate, keys, values)]
    return pl.pallas_call(
        rest_states_kernel,
        in_specs=[SMEM, HBM, HBM, HBM],
        out_specs=[VMEM] * 4,
        out_shape=[pltpu.VMEM((2 * HALF, SLICE, DK), jnp.float32)]
        + [pltpu.VMEM((tokens, EARLY * LANES), kind) for kind in kinds],
        scratch_shapes=[pltpu.VMEM((tokens, WIDTH), kind) for kind in kinds]
        + [pltpu.SemaphoreType.DMA((3 * STEPS,)), pltpu.SemaphoreType.DMA((3 * EARLY,))],
        compiler_params=pltpu.CompilerParams(vmem_limit_bytes=8 << 20),
        cost_estimate=pl.CostEstimate(flops=10**9, bytes_accessed=9 * 10**6, transcendentals=10**6),
        name="rest_states",
    )(core, in_hbm(gate), in_hbm(keys), in_hbm(values))


def own_states_kernel(
    core_ref, gate_hbm, key_hbm, value_hbm, early_gate, early_key, early_value, out_ref, gate, key, value, sems
):
    mine = column_copies(
        core_ref[0], range(EARLY, STEPS), (gate_hbm, key_hbm, value_hbm), (gate, key, value), sems
    )
    for copies in mine:
        start_all(copies)
    for step in range(EARLY):
        states_step(step, early_gate, early_key, early_value, out_ref)
    for step in range(EARLY, STEPS):
        wait_all(mine[step - EARLY])
        states_step(step, gate, key, value, out_ref)


def own_states(core, gate, keys, values, early):
    tokens = keys.shape[0]
    kinds = [x.dtype for x in (gate, keys, values)]
    return pl.pallas_call(
        own_states_kernel,
        in_specs=[SMEM, HBM, HBM, HBM] + [VMEM] * 3,
        out_specs=VMEM,
        out_shape=pltpu.VMEM((2 * HALF, SLICE, DK), jnp.float32),
        scratch_shapes=[pltpu.VMEM((tokens, WIDTH), kind) for kind in kinds]
        + [pltpu.SemaphoreType.DMA((3 * (STEPS - EARLY),))],
        compiler_params=pltpu.CompilerParams(vmem_limit_bytes=8 << 20),
        cost_estimate=pl.CostEstimate(flops=10**9, bytes_accessed=5 * 10**6, transcendentals=10**6),
        name="own_states",
    )(core, in_hbm(gate), in_hbm(keys), in_hbm(values), *map(in_vmem, early))


def combine_kernel(core_ref, mine_ref, other_ref, out_ref, keep_ref):
    first = core_ref[0] == 0
    mine_total = mine_ref[:, ROWS:SLICE, :]
    other_total = other_ref[:, ROWS:SLICE, :]
    mine_weight = jnp.where(first, jnp.exp2(other_total), 1.0)[:, 0:1]
    other_weight = jnp.where(first, 1.0, jnp.exp2(mine_total))[:, 0:1]
    mine = mine_ref[:, 0:ROWS, :]
    other = other_ref[:, 0:ROWS, :]
    out_ref[:, 0:ROWS, :] = mine * mine_weight + other * other_weight
    out_ref[:, ROWS:SLICE, :] = mine_total + other_total
    keep_ref[:, 0:ROWS, :] = jnp.where(first, mine, other)
    keep_ref[:, ROWS:SLICE, :] = jnp.where(first, mine_total, other_total)


def combine(core, mine, other):
    return pl.pallas_call(
        combine_kernel,
        in_specs=[SMEM, VMEM, VMEM],
        out_specs=[VMEM, VMEM],
        out_shape=[pltpu.VMEM(mine.shape, jnp.float32)] * 2,
        compiler_params=pltpu.CompilerParams(vmem_limit_bytes=4 << 20),
        name="combine",
    )(core, in_vmem(mine), in_vmem(other))


def advance_kernel(core_ref, entry_ref, keep_ref, mine_ref, sent_ref):
    first = core_ref[0] == 0
    entry = entry_ref[...]
    advanced = entry * jnp.exp2(keep_ref[:, ROWS : ROWS + 1, :]) + keep_ref[:, 0:ROWS, :]
    mine_ref[...] = jnp.where(first, entry, advanced)
    sent_ref[...] = jnp.where(first, advanced, entry)


def advance(core, entry, keep):
    return pl.pallas_call(
        advance_kernel,
        in_specs=[SMEM, VMEM, VMEM],
        out_specs=[VMEM, VMEM],
        out_shape=[pltpu.VMEM(entry.shape, jnp.float32)] * 2,
        compiler_params=pltpu.CompilerParams(vmem_limit_bytes=4 << 20),
        name="advance",
    )(core, in_vmem(entry), in_vmem(keep))


def prefix_kernel(in_ref, out_hbm, done_ref, out_ref, sems):
    done_ref[...] = jnp.zeros_like(done_ref)
    running = jnp.zeros((ROWS, DK), jnp.float32)
    chips = in_ref.shape[0]
    copies = []
    for chip in range(chips):
        out_ref[chip] = running
        if (chip + 1) % CHUNKS == 0:
            at = pl.ds(chip + 1 - CHUNKS, CHUNKS)
            copies.append(pltpu.make_async_copy(out_ref.at[at], out_hbm.at[at], sems.at[len(copies)]))
            copies[-1].start()
        if chip < chips - 1:
            decay = jnp.exp2(in_ref[chip, ROWS : ROWS + 1, :])
            running = running * decay + in_ref[chip, 0:ROWS, :]
    wait_all(copies)


def prefix(received):
    shape = (received.shape[0], ROWS, DK)
    return pl.pallas_call(
        prefix_kernel,
        in_specs=[VMEM],
        out_specs=[HBM, VMEM],
        out_shape=[pltpu.HBM(shape, jnp.float32), jax.ShapeDtypeStruct((8, DK), jnp.float32)],
        scratch_shapes=[pltpu.VMEM(shape, jnp.float32), pltpu.SemaphoreType.DMA((shape[0] // CHUNKS,))],
        compiler_params=pltpu.CompilerParams(vmem_limit_bytes=4 << 20),
        name="prefix",
    )(in_vmem(received))


def local_step(step, waits, query_ref, key_ref, value_ref, gate_ref, local_ref, decayed_ref, stored):
    ones = triangle(False)
    row = lax.broadcasted_iota(jnp.int32, (GROUP, GROUP), 0)
    col = lax.broadcasted_iota(jnp.int32, (GROUP, GROUP), 1)
    causal = row >= col
    cols = pl.ds(step * WIDE, WIDE)
    groups = range(gate_ref.shape[0] // GROUP)
    heads = range(WIDE // DK)
    rows = [pl.ds(group * GROUP, GROUP) for group in groups]
    at = [slice(head * DK, (head + 1) * DK) for head in heads]
    waits[0]()
    sums = [partial_sums(ones, gate_ref[rows[group], cols] * LOG2E) for group in groups]
    gamma = [inclusive[GROUP - 1 : GROUP] for inclusive in sums]
    decay = [jnp.exp2(total) for total in gamma]
    waits[1]()
    queries, keys, to_end = [], [], []
    before = None
    for group in groups:
        query = query_ref[rows[group], cols].astype(jnp.float32) * jnp.exp2(sums[group] + LOG2_SCALE)
        key = key_ref[rows[group], cols].astype(jnp.float32) * jnp.exp2(-sums[group])
        queries.append(query.astype(jnp.bfloat16))
        keys.append(key.astype(jnp.bfloat16))
        to_end.append((key * decay[group]).astype(jnp.bfloat16))
        if group == 0:
            decayed_ref[rows[group], cols] = queries[group]
            before = gamma[group]
        else:
            decayed_ref[rows[group], cols] = (query * jnp.exp2(before)).astype(jnp.bfloat16)
            before = before + gamma[group]
    stored(0, cols)
    value_cols = [pl.ds(step * WIDE + head * DV, DV) for head in heads]
    scores = [[dot(queries[group][:, at[head]], keys[group][:, at[head]], NT) for head in heads] for group in groups]
    scores = [[jnp.where(causal, x, 0.0).astype(jnp.bfloat16) for x in line] for line in scores]
    updates = [
        [dot(value_ref[rows[group], value_cols[head]], to_end[group][:, at[head]], TN) for head in heads]
        for group in groups[:-1]
    ]
    for head in heads:
        state = None
        for group in groups:
            value = value_ref[rows[group], value_cols[head]]
            if group == 0:
                out = dot(scores[group][head], value)
                state = updates[group][head]
            else:
                left = jnp.concatenate([scores[group][head], queries[group][:, at[head]]], axis=1)
                out = dot(left, jnp.concatenate([value, state.astype(jnp.bfloat16).T], axis=0))
                if group < groups[-1]:
                    state = state * decay[group][:, at[head]] + updates[group][head]
            local_ref[rows[group], value_cols[head]] = out.astype(local_ref.dtype)
    stored(1, cols)


def local_kernel(*refs):
    core_ref, query_hbm, key_hbm, value_hbm, gate_hbm, _ = refs[:6]
    own_local, own_decayed, rest_local_hbm, rest_decayed_hbm, done_ref = refs[6:11]
    query, key, value, gate, rest_local, rest_decayed, first, sems, first_sem, store_sems = refs[11:]
    core = core_ref[0]
    steps = range(LOCAL_STEPS)
    queue = []
    for i, half in ((0, core), (1, 1 - core)):
        targets = tuple(x.at[i] for x in (gate, key, query, value))
        queue += column_copies(half, steps, (gate_hbm, key_hbm, query_hbm, value_hbm), targets, sems.at[i], WIDE)
    early = pltpu.make_async_copy(gate_hbm.at[0:8, 0:DK], first, first_sem)
    early.start()
    start_all(queue[0])
    early.wait()
    start_all(queue[1])
    stores = []

    def store(which, cols):
        ref, out = ((rest_decayed, rest_decayed_hbm), (rest_local, rest_local_hbm))[which]
        stores.append(pltpu.make_async_copy(ref.at[:, cols], out.at[:, cols], store_sems.at[len(stores)]))
        stores[-1].start()

    for i, out, decayed, stored in (
        (0, own_local, own_decayed, lambda which, cols: None),
        (1, rest_local, rest_decayed, store),
    ):
        inputs = [x.at[i] for x in (query, key, value, gate)]
        for step in steps:
            place = i * LOCAL_STEPS + step

            def gates(place=place):
                queue[place][0].wait()
                if place + 2 < len(queue):
                    start_all(queue[place + 2])

            local_step(step, (gates, lambda place=place: wait_all(queue[place][1:])), *inputs, out, decayed, stored)
    done_ref[...] = jnp.zeros_like(done_ref)
    wait_all(stores)


def local_part(core, queries, keys, values, gate, after):
    tokens = keys.shape[0]
    half = ((tokens, WIDTH), jnp.bfloat16)
    return pl.pallas_call(
        local_kernel,
        in_specs=[SMEM] + [HBM] * 4 + [ANY],
        out_specs=[VMEM, VMEM, HBM, HBM, VMEM],
        out_shape=[pltpu.VMEM(*half)] * 2 + [pltpu.HBM(*half)] * 2 + [jax.ShapeDtypeStruct((8, DK), jnp.float32)],
        scratch_shapes=[pltpu.VMEM((2, tokens, WIDTH), x.dtype) for x in (queries, keys, values, gate)]
        + [pltpu.VMEM(*half)] * 2
        + [pltpu.VMEM((8, DK), jnp.float32), pltpu.SemaphoreType.DMA((2, 4 * LOCAL_STEPS))]
        + [pltpu.SemaphoreType.DMA, pltpu.SemaphoreType.DMA((2 * LOCAL_STEPS,))],
        compiler_params=pltpu.CompilerParams(vmem_limit_bytes=32 << 20),
        cost_estimate=pl.CostEstimate(flops=8 * 10**9, bytes_accessed=16 * 10**6, transcendentals=10**6),
        name="local_part",
    )(core, in_hbm(queries), in_hbm(keys), in_hbm(values), in_hbm(gate), after)


def final_step(step, local_ref, decayed_ref, entry_ref, out_ref):
    for head in range(step * HEADS_STEP, (step + 1) * HEADS_STEP):
        at = slice(head * DK, (head + 1) * DK)
        across = dot(decayed_ref[:, at], entry_ref[at, :].astype(jnp.bfloat16), NT)
        out_ref[:, at] = (local_ref[:, at].astype(jnp.float32) + across).astype(jnp.bfloat16)


def final_steps(half, local_ref, decayed_ref, entry_ref, out_hbm, out_ref, sems):
    copies = []
    for step in range(STEPS):
        final_step(step, local_ref, decayed_ref, entry_ref, out_ref)
        at = pl.ds(step * LANES, LANES)
        copies.append(pltpu.make_async_copy(out_ref.at[:, at], out_hbm.at[:, columns(half, step)], sems.at[step]))
        copies[-1].start()
    wait_all(copies)


def own_final_kernel(core_ref, local, decayed, entry, local_hbm, decayed_hbm, _, out_hbm, rest_local, rest_decayed, *refs):
    out_ref, sems, fetch_sems = refs
    fetches = [
        pltpu.make_async_copy(local_hbm, rest_local, fetch_sems.at[0]),
        pltpu.make_async_copy(decayed_hbm, rest_decayed, fetch_sems.at[1]),
    ]
    for fetch in fetches:
        fetch.start()
    final_steps(core_ref[0], local, decayed, entry, out_hbm, out_ref, sems)
    wait_all(fetches)


def own_final(core, local, decayed, entry, rest_local, rest_decayed, after):
    tokens = local.shape[0]
    return pl.pallas_call(
        own_final_kernel,
        in_specs=[SMEM] + [VMEM] * 3 + [HBM] * 2 + [ANY],
        out_specs=[HBM, VMEM, VMEM],
        out_shape=[jax.ShapeDtypeStruct((tokens, H * DV), jnp.bfloat16)]
        + [pltpu.VMEM(x.shape, x.dtype) for x in (rest_local, rest_decayed)],
        scratch_shapes=[
            pltpu.VMEM((tokens, WIDTH), jnp.bfloat16),
            pltpu.SemaphoreType.DMA((STEPS,)),
            pltpu.SemaphoreType.DMA((2,)),
        ],
        compiler_params=pltpu.CompilerParams(vmem_limit_bytes=8 << 20),
        cost_estimate=pl.CostEstimate(flops=10**9, bytes_accessed=4 * 10**6, transcendentals=0),
        name="own_final",
    )(core, *map(in_vmem, (local, decayed, entry)), in_hbm(rest_local), in_hbm(rest_decayed), after)


def rest_final_kernel(core_ref, local, decayed, entry, _, out_hbm, out_ref, sems):
    final_steps(1 - core_ref[0], local, decayed, entry, out_hbm, out_ref, sems)


def rest_final(core, local, decayed, entry, out):
    tokens = local.shape[0]
    return pl.pallas_call(
        rest_final_kernel,
        in_specs=[SMEM] + [VMEM] * 3 + [ANY],
        out_specs=HBM,
        out_shape=jax.ShapeDtypeStruct((tokens, H * DV), jnp.bfloat16),
        input_output_aliases={4: 0},
        scratch_shapes=[pltpu.VMEM((tokens, WIDTH), jnp.bfloat16), pltpu.SemaphoreType.DMA((STEPS,))],
        compiler_params=pltpu.CompilerParams(vmem_limit_bytes=8 << 20),
        cost_estimate=pl.CostEstimate(flops=10**9, bytes_accessed=4 * 10**6, transcendentals=0),
        name="rest_final",
    )(core, *map(in_vmem, (local, decayed, entry)), out)


def on_device(queries, keys, values, log_gate):
    devices = lax.axis_size("seq")
    chips = devices // 2
    core = lax.rem(lax.axis_index("seq"), 2).astype(jnp.int32)[None]
    swap = [(i, i ^ 1) for i in range(devices)]
    same_core = [[2 * chip + c for chip in range(chips)] for c in range(2)]

    def exchange(blocks):
        return lax.all_to_all(blocks, "seq", split_axis=0, concat_axis=0, axis_index_groups=same_core, tiled=True)

    rest, *early = rest_states(core, log_gate, keys, values)
    own_other = lax.ppermute(rest, "seq", swap)
    own = own_states(core, log_gate, keys, values, early)
    combined, keep = combine(core, own, own_other)
    entries, after = prefix(exchange(combined))
    entry = exchange(entries)
    own_local, own_decayed, rest_local, rest_decayed, after = local_part(core, queries, keys, values, log_gate, after)
    entry, after = lax.optimization_barrier((entry, after))
    own_entry, sent = advance(core, entry, keep)
    rest_entry = lax.ppermute(sent, "seq", swap).reshape(HALF * DV, DK)
    own_entry = own_entry.reshape(HALF * DV, DK)
    out, local, decayed = own_final(core, own_local, own_decayed, own_entry, rest_local, rest_decayed, after)
    return rest_final(core, local, decayed, rest_entry, out)


def solution(mesh):
    spec = P(("batch", "seq"), None)
    return jax.shard_map(on_device, mesh=mesh, in_specs=(spec,) * 4, out_specs=spec, check_vma=False)
```

```python
import functools
import math

import jax
import jax.numpy as jnp
from jax import lax
from jax.experimental import pallas as pl
from jax.experimental.pallas import tpu as pltpu
from jax.sharding import PartitionSpec as P

H = 16
DK = 128
DV = 128
GROUP = 128
HALF = H // 2
WIDTH = HALF * DK
HEADS_STEP = 2
LANES = HEADS_STEP * DK
STEPS = HALF // HEADS_STEP
EARLY = 2
WIDE = 512
LOCAL_STEPS = WIDTH // WIDE
CHUNK = 1
IN_FIRST = 10
OUT_FIRST = 14
ROWS = 64
SLICE = ROWS + 8
LOG2E = math.log2(math.e)
LOG2_SCALE = -0.5 * math.log2(DK)

NT = (((1,), (1,)), ((), ()))
TN = (((0,), (0,)), ((), ()))

VMEM = pl.BlockSpec(memory_space=pltpu.VMEM)
SMEM = pl.BlockSpec(memory_space=pltpu.SMEM)
HBM = pl.BlockSpec(memory_space=pltpu.HBM)
ANY = pl.BlockSpec(memory_space=pl.ANY)


def in_vmem(x):
    return pltpu.with_memory_space_constraint(x, pltpu.VMEM)


def in_hbm(x):
    return pltpu.with_memory_space_constraint(x, pltpu.HBM)


def dot(a, b, dims=(((1,), (0,)), ((), ()))):
    return lax.dot_general(a, b, dims, preferred_element_type=jnp.float32)


def triangle(strict_upper):
    row = lax.broadcasted_iota(jnp.int32, (GROUP, 2 * GROUP), 0)
    col = lax.broadcasted_iota(jnp.int32, (GROUP, 2 * GROUP), 1)
    col = jnp.where(col >= GROUP, col - GROUP, col)
    keep = col > row if strict_upper else col <= row
    return jnp.where(keep, 1.0, 0.0).astype(jnp.bfloat16)


def partial_sums(ones, gate):
    high = gate.astype(jnp.bfloat16)
    low = (gate - high.astype(jnp.float32)).astype(jnp.bfloat16)
    return dot(ones, jnp.concatenate([high, low], axis=0))


def columns(half, step, lanes=LANES):
    return pl.ds(pl.multiple_of(half * WIDTH + step * lanes, lanes), lanes)


def states_step(step, gate_ref, key_ref, value_ref, out_ref):
    ones = triangle(True)
    state = [jnp.zeros((DV, DK), jnp.float32)] * HEADS_STEP
    total = [jnp.zeros((1, DK), jnp.float32)] * HEADS_STEP
    cols = pl.ds(step * LANES, LANES)
    for group in range(gate_ref.shape[0] // GROUP):
        rows = pl.ds(group * GROUP, GROUP)
        gate = gate_ref[rows, cols] * LOG2E
        later = partial_sums(ones, gate)
        gamma = later[0:1] + gate[0:1]
        to_end = (key_ref[rows, cols].astype(jnp.float32) * jnp.exp2(later)).astype(jnp.bfloat16)
        decay = jnp.exp2(gamma)
        for head in range(HEADS_STEP):
            at = slice(head * DK, (head + 1) * DK)
            value = value_ref[rows, pl.ds(step * LANES + head * DV, DV)]
            state[head] = state[head] * decay[:, at] + dot(value, to_end[:, at], TN)
            total[head] = total[head] + gamma[:, at]
    for head in range(HEADS_STEP):
        for part in range(2):
            at = 2 * (step * HEADS_STEP + head) + part
            out_ref[at, 0:ROWS, :] = state[head][ROWS * part : ROWS * (part + 1)]
            out_ref[at, ROWS:SLICE, :] = jnp.broadcast_to(total[head], (SLICE - ROWS, DK))


def column_copies(half, steps, sources, targets, sems, lanes=LANES):
    copies = []
    for step in steps:
        for source, target in zip(sources, targets):
            at = pl.ds(step * lanes, lanes)
            copies.append(
                pltpu.make_async_copy(source.at[:, columns(half, step, lanes)], target.at[:, at], sems.at[len(copies)])
            )
    return [copies[i : i + len(sources)] for i in range(0, len(copies), len(sources))]


def start_all(copies):
    for copy in copies:
        copy.start()


def wait_all(copies):
    for copy in copies:
        copy.wait()


def rest_states_kernel(
    core_ref, gate_hbm, key_hbm, value_hbm, out_ref, own_gate, own_key, own_value, gate, key, value, sems, own_sems
):
    sources = (gate_hbm, key_hbm, value_hbm)
    mine = column_copies(1 - core_ref[0], range(STEPS), sources, (gate, key, value), sems)
    early = column_copies(core_ref[0], range(EARLY), sources, (own_gate, own_key, own_value), own_sems)
    for copies in mine + early:
        start_all(copies)
    for step in range(STEPS):
        wait_all(mine[step])
        states_step(step, gate, key, value, out_ref)
    for copies in early:
        wait_all(copies)


def rest_states(core, gate, keys, values):
    tokens = keys.shape[0]
    kinds = [x.dtype for x in (gate, keys, values)]
    return pl.pallas_call(
        rest_states_kernel,
        in_specs=[SMEM, HBM, HBM, HBM],
        out_specs=[VMEM] * 4,
        out_shape=[pltpu.VMEM((2 * HALF, SLICE, DK), jnp.float32)]
        + [pltpu.VMEM((tokens, EARLY * LANES), kind) for kind in kinds],
        scratch_shapes=[pltpu.VMEM((tokens, WIDTH), kind) for kind in kinds]
        + [pltpu.SemaphoreType.DMA((3 * STEPS,)), pltpu.SemaphoreType.DMA((3 * EARLY,))],
        compiler_params=pltpu.CompilerParams(vmem_limit_bytes=8 << 20),
        cost_estimate=pl.CostEstimate(flops=10**9, bytes_accessed=9 * 10**6, transcendentals=10**6),
        name="rest_states",
    )(core, in_hbm(gate), in_hbm(keys), in_hbm(values))


def own_states_kernel(
    core_ref, gate_hbm, key_hbm, value_hbm, early_gate, early_key, early_value, out_ref, gate, key, value, sems
):
    mine = column_copies(
        core_ref[0], range(EARLY, STEPS), (gate_hbm, key_hbm, value_hbm), (gate, key, value), sems
    )
    for copies in mine:
        start_all(copies)
    for step in range(EARLY):
        states_step(step, early_gate, early_key, early_value, out_ref)
    for step in range(EARLY, STEPS):
        wait_all(mine[step - EARLY])
        states_step(step, gate, key, value, out_ref)


def own_states(core, gate, keys, values, early):
    tokens = keys.shape[0]
    kinds = [x.dtype for x in (gate, keys, values)]
    return pl.pallas_call(
        own_states_kernel,
        in_specs=[SMEM, HBM, HBM, HBM] + [VMEM] * 3,
        out_specs=VMEM,
        out_shape=pltpu.VMEM((2 * HALF, SLICE, DK), jnp.float32),
        scratch_shapes=[pltpu.VMEM((tokens, WIDTH), kind) for kind in kinds]
        + [pltpu.SemaphoreType.DMA((3 * (STEPS - EARLY),))],
        compiler_params=pltpu.CompilerParams(vmem_limit_bytes=8 << 20),
        cost_estimate=pl.CostEstimate(flops=10**9, bytes_accessed=5 * 10**6, transcendentals=10**6),
        name="own_states",
    )(core, in_hbm(gate), in_hbm(keys), in_hbm(values), *map(in_vmem, early))


def combine_kernel(core_ref, mine_ref, other_ref, out_ref, keep_ref):
    first = core_ref[0] == 0
    mine_total = mine_ref[:, ROWS:SLICE, :]
    other_total = other_ref[:, ROWS:SLICE, :]
    mine_weight = jnp.where(first, jnp.exp2(other_total), 1.0)[:, 0:1]
    other_weight = jnp.where(first, 1.0, jnp.exp2(mine_total))[:, 0:1]
    mine = mine_ref[:, 0:ROWS, :]
    other = other_ref[:, 0:ROWS, :]
    out_ref[:, 0:ROWS, :] = mine * mine_weight + other * other_weight
    out_ref[:, ROWS:SLICE, :] = mine_total + other_total
    keep_ref[:, 0:ROWS, :] = jnp.where(first, mine, other)
    keep_ref[:, ROWS:SLICE, :] = jnp.where(first, mine_total, other_total)


def combine(core, mine, other):
    return pl.pallas_call(
        combine_kernel,
        in_specs=[SMEM, VMEM, VMEM],
        out_specs=[VMEM, VMEM],
        out_shape=[pltpu.VMEM(mine.shape, jnp.float32)] * 2,
        compiler_params=pltpu.CompilerParams(vmem_limit_bytes=4 << 20),
        name="combine",
    )(core, in_vmem(mine), in_vmem(other))


def advance_kernel(core_ref, entry_ref, keep_ref, mine_ref, sent_ref):
    first = core_ref[0] == 0
    chips = entry_ref.shape[0]
    for at in range(chips):
        entry = entry_ref[(at + IN_FIRST - OUT_FIRST) % chips]
        advanced = entry * jnp.exp2(keep_ref[at, ROWS : ROWS + 1, :]) + keep_ref[at, 0:ROWS, :]
        mine_ref[at] = jnp.where(first, entry, advanced)
        sent_ref[at] = jnp.where(first, advanced, entry)


def advance(core, entry, keep):
    return pl.pallas_call(
        advance_kernel,
        in_specs=[SMEM, VMEM, VMEM],
        out_specs=[VMEM, VMEM],
        out_shape=[pltpu.VMEM(entry.shape, jnp.float32)] * 2,
        compiler_params=pltpu.CompilerParams(vmem_limit_bytes=4 << 20),
        name="advance",
    )(core, in_vmem(entry), in_vmem(keep))


def prefix_kernel(in_ref, out_hbm, done_ref, out_ref, sems):
    done_ref[...] = jnp.zeros_like(done_ref)
    running = jnp.zeros((ROWS, DK), jnp.float32)
    chips = in_ref.shape[0]
    copies = []
    for chip in range(chips):
        out_ref[(chip - OUT_FIRST) % chips] = running
        if chip % CHUNK == CHUNK - 1:
            at = pl.ds((chip + 1 - CHUNK - OUT_FIRST) % chips, CHUNK)
            copies.append(pltpu.make_async_copy(out_ref.at[at], out_hbm.at[at], sems.at[len(copies)]))
            copies[-1].start()
        if chip < chips - 1:
            place = (chip - IN_FIRST) % chips
            decay = jnp.exp2(in_ref[place, ROWS : ROWS + 1, :])
            running = running * decay + in_ref[place, 0:ROWS, :]
    wait_all(copies)


def prefix(received):
    shape = (received.shape[0], ROWS, DK)
    return pl.pallas_call(
        prefix_kernel,
        in_specs=[VMEM],
        out_specs=[HBM, VMEM],
        out_shape=[pltpu.HBM(shape, jnp.float32), jax.ShapeDtypeStruct((8, DK), jnp.float32)],
        scratch_shapes=[pltpu.VMEM(shape, jnp.float32), pltpu.SemaphoreType.DMA((shape[0] // CHUNK,))],
        compiler_params=pltpu.CompilerParams(vmem_limit_bytes=4 << 20),
        name="prefix",
    )(in_vmem(received))


def local_step(step, waits, query_ref, key_ref, value_ref, gate_ref, local_ref, decayed_ref, stored):
    ones = triangle(False)
    row = lax.broadcasted_iota(jnp.int32, (GROUP, GROUP), 0)
    col = lax.broadcasted_iota(jnp.int32, (GROUP, GROUP), 1)
    causal = row >= col
    cols = pl.ds(step * WIDE, WIDE)
    groups = range(gate_ref.shape[0] // GROUP)
    heads = range(WIDE // DK)
    rows = [pl.ds(group * GROUP, GROUP) for group in groups]
    at = [slice(head * DK, (head + 1) * DK) for head in heads]
    waits[0]()
    sums = [partial_sums(ones, gate_ref[rows[group], cols] * LOG2E) for group in groups]
    gamma = [inclusive[GROUP - 1 : GROUP] for inclusive in sums]
    decay = [jnp.exp2(total) for total in gamma]
    waits[1]()
    queries, keys, to_end = [], [], []
    before = None
    for group in groups:
        query = query_ref[rows[group], cols].astype(jnp.float32) * jnp.exp2(sums[group] + LOG2_SCALE)
        key = key_ref[rows[group], cols].astype(jnp.float32) * jnp.exp2(-sums[group])
        queries.append(query.astype(jnp.bfloat16))
        keys.append(key.astype(jnp.bfloat16))
        to_end.append((key * decay[group]).astype(jnp.bfloat16))
        if group == 0:
            decayed_ref[rows[group], cols] = queries[group]
            before = gamma[group]
        else:
            decayed_ref[rows[group], cols] = (query * jnp.exp2(before)).astype(jnp.bfloat16)
            before = before + gamma[group]
    stored(0, cols)
    value_cols = [pl.ds(step * WIDE + head * DV, DV) for head in heads]
    scores = [[dot(queries[group][:, at[head]], keys[group][:, at[head]], NT) for head in heads] for group in groups]
    scores = [[jnp.where(causal, x, 0.0).astype(jnp.bfloat16) for x in line] for line in scores]
    updates = [
        [dot(value_ref[rows[group], value_cols[head]], to_end[group][:, at[head]], TN) for head in heads]
        for group in groups[:-1]
    ]
    for head in heads:
        state = None
        for group in groups:
            value = value_ref[rows[group], value_cols[head]]
            if group == 0:
                out = dot(scores[group][head], value)
                state = updates[group][head]
            else:
                left = jnp.concatenate([scores[group][head], queries[group][:, at[head]]], axis=1)
                out = dot(left, jnp.concatenate([value, state.astype(jnp.bfloat16).T], axis=0))
                if group < groups[-1]:
                    state = state * decay[group][:, at[head]] + updates[group][head]
            local_ref[rows[group], value_cols[head]] = out.astype(local_ref.dtype)
    stored(1, cols)


def local_kernel(*refs):
    core_ref, query_hbm, key_hbm, value_hbm, gate_hbm, _ = refs[:6]
    own_local, own_decayed, rest_local_hbm, rest_decayed_hbm, done_ref = refs[6:11]
    query, key, value, gate, rest_local, rest_decayed, first, sems, first_sem, store_sems = refs[11:]
    core = core_ref[0]
    steps = range(LOCAL_STEPS)
    queue = []
    for i, half in ((0, 1 - core), (1, core)):
        targets = tuple(x.at[i] for x in (gate, key, query, value))
        queue += column_copies(half, steps, (gate_hbm, key_hbm, query_hbm, value_hbm), targets, sems.at[i], WIDE)
    early = pltpu.make_async_copy(gate_hbm.at[0:8, 0:DK], first, first_sem)
    early.start()
    start_all(queue[0])
    early.wait()
    start_all(queue[1])
    stores = []

    def store(which, cols):
        ref, out = ((rest_decayed, rest_decayed_hbm), (rest_local, rest_local_hbm))[which]
        stores.append(pltpu.make_async_copy(ref.at[:, cols], out.at[:, cols], store_sems.at[len(stores)]))
        stores[-1].start()

    for i, out, decayed, stored in (
        (0, rest_local, rest_decayed, store),
        (1, own_local, own_decayed, lambda which, cols: None),
    ):
        inputs = [x.at[i] for x in (query, key, value, gate)]
        for step in steps:
            place = i * LOCAL_STEPS + step

            def gates(place=place):
                queue[place][0].wait()
                if place + 2 < len(queue):
                    start_all(queue[place + 2])

            local_step(step, (gates, lambda place=place: wait_all(queue[place][1:])), *inputs, out, decayed, stored)
    done_ref[...] = jnp.zeros_like(done_ref)
    wait_all(stores)


def local_part(core, queries, keys, values, gate, after):
    tokens = keys.shape[0]
    half = ((tokens, WIDTH), jnp.bfloat16)
    return pl.pallas_call(
        local_kernel,
        in_specs=[SMEM] + [HBM] * 4 + [ANY],
        out_specs=[VMEM, VMEM, HBM, HBM, VMEM],
        out_shape=[pltpu.VMEM(*half)] * 2 + [pltpu.HBM(*half)] * 2 + [jax.ShapeDtypeStruct((8, DK), jnp.float32)],
        scratch_shapes=[pltpu.VMEM((2, tokens, WIDTH), x.dtype) for x in (queries, keys, values, gate)]
        + [pltpu.VMEM(*half)] * 2
        + [pltpu.VMEM((8, DK), jnp.float32), pltpu.SemaphoreType.DMA((2, 4 * LOCAL_STEPS))]
        + [pltpu.SemaphoreType.DMA, pltpu.SemaphoreType.DMA((2 * LOCAL_STEPS,))],
        compiler_params=pltpu.CompilerParams(vmem_limit_bytes=32 << 20),
        cost_estimate=pl.CostEstimate(flops=8 * 10**9, bytes_accessed=16 * 10**6, transcendentals=10**6),
        name="local_part",
    )(core, in_hbm(queries), in_hbm(keys), in_hbm(values), in_hbm(gate), after)


def final_step(step, local_ref, decayed_ref, entry_ref, out_ref):
    for head in range(step * HEADS_STEP, (step + 1) * HEADS_STEP):
        at = slice(head * DK, (head + 1) * DK)
        across = dot(decayed_ref[:, at], entry_ref[at, :].astype(jnp.bfloat16), NT)
        out_ref[:, at] = (local_ref[:, at].astype(jnp.float32) + across).astype(jnp.bfloat16)


def final_steps(half, local_ref, decayed_ref, entry_ref, out_hbm, out_ref, sems):
    copies = []
    for step in range(STEPS):
        final_step(step, local_ref, decayed_ref, entry_ref, out_ref)
        at = pl.ds(step * LANES, LANES)
        copies.append(pltpu.make_async_copy(out_ref.at[:, at], out_hbm.at[:, columns(half, step)], sems.at[step]))
        copies[-1].start()
    wait_all(copies)


def own_final_kernel(core_ref, local, decayed, entry, local_hbm, decayed_hbm, _, out_hbm, rest_local, rest_decayed, *refs):
    out_ref, sems, fetch_sems = refs
    fetches = [
        pltpu.make_async_copy(local_hbm, rest_local, fetch_sems.at[0]),
        pltpu.make_async_copy(decayed_hbm, rest_decayed, fetch_sems.at[1]),
    ]
    for fetch in fetches:
        fetch.start()
    final_steps(core_ref[0], local, decayed, entry, out_hbm, out_ref, sems)
    wait_all(fetches)


def own_final(core, local, decayed, entry, rest_local, rest_decayed, after):
    tokens = local.shape[0]
    return pl.pallas_call(
        own_final_kernel,
        in_specs=[SMEM] + [VMEM] * 3 + [HBM] * 2 + [ANY],
        out_specs=[HBM, VMEM, VMEM],
        out_shape=[jax.ShapeDtypeStruct((tokens, H * DV), jnp.bfloat16)]
        + [pltpu.VMEM(x.shape, x.dtype) for x in (rest_local, rest_decayed)],
        scratch_shapes=[
            pltpu.VMEM((tokens, WIDTH), jnp.bfloat16),
            pltpu.SemaphoreType.DMA((STEPS,)),
            pltpu.SemaphoreType.DMA((2,)),
        ],
        compiler_params=pltpu.CompilerParams(vmem_limit_bytes=8 << 20),
        cost_estimate=pl.CostEstimate(flops=10**9, bytes_accessed=4 * 10**6, transcendentals=0),
        name="own_final",
    )(core, *map(in_vmem, (local, decayed, entry)), in_hbm(rest_local), in_hbm(rest_decayed), after)


def rest_final_kernel(core_ref, local, decayed, entry, _, out_hbm, out_ref, sems):
    final_steps(1 - core_ref[0], local, decayed, entry, out_hbm, out_ref, sems)


def rest_final(core, local, decayed, entry, out):
    tokens = local.shape[0]
    return pl.pallas_call(
        rest_final_kernel,
        in_specs=[SMEM] + [VMEM] * 3 + [ANY],
        out_specs=HBM,
        out_shape=jax.ShapeDtypeStruct((tokens, H * DV), jnp.bfloat16),
        input_output_aliases={4: 0},
        scratch_shapes=[pltpu.VMEM((tokens, WIDTH), jnp.bfloat16), pltpu.SemaphoreType.DMA((STEPS,))],
        compiler_params=pltpu.CompilerParams(vmem_limit_bytes=8 << 20),
        cost_estimate=pl.CostEstimate(flops=10**9, bytes_accessed=4 * 10**6, transcendentals=0),
        name="rest_final",
    )(core, *map(in_vmem, (local, decayed, entry)), out)


def on_device(queries, keys, values, log_gate):
    devices = lax.axis_size("seq")
    chips = devices // 2
    core = lax.rem(lax.axis_index("seq"), 2).astype(jnp.int32)[None]
    swap = [(i, i ^ 1) for i in range(devices)]

    def exchange(blocks, first):
        same_core = [[2 * ((place + first) % chips) + c for place in range(chips)] for c in range(2)]
        return lax.all_to_all(blocks, "seq", split_axis=0, concat_axis=0, axis_index_groups=same_core, tiled=True)

    rest, *early = rest_states(core, log_gate, keys, values)
    own_other = lax.ppermute(rest, "seq", swap)
    own = own_states(core, log_gate, keys, values, early)
    combined, keep = combine(core, own, own_other)
    entries, after = prefix(exchange(combined, IN_FIRST))
    entry = exchange(entries, OUT_FIRST)
    own_local, own_decayed, rest_local, rest_decayed, after = local_part(core, queries, keys, values, log_gate, after)
    entry, after = lax.optimization_barrier((entry, after))
    own_entry, sent = advance(core, entry, keep)
    rest_entry = lax.ppermute(sent, "seq", swap).reshape(HALF * DV, DK)
    own_entry = own_entry.reshape(HALF * DV, DK)
    out, local, decayed = own_final(core, own_local, own_decayed, own_entry, rest_local, rest_decayed, after)
    return rest_final(core, local, decayed, rest_entry, out)


def solution(mesh):
    spec = P(("batch", "seq"), None)
    return jax.shard_map(on_device, mesh=mesh, in_specs=(spec,) * 4, out_specs=spec, check_vma=False)
```

```python
import functools
import math

import jax
import jax.numpy as jnp
from jax import lax
from jax.experimental import pallas as pl
from jax.experimental.pallas import tpu as pltpu
from jax.sharding import PartitionSpec as P

H = 16
DK = 128
DV = 128
GROUP = 128
HALF = H // 2
WIDTH = HALF * DK
HEADS_STEP = 2
LANES = HEADS_STEP * DK
STEPS = HALF // HEADS_STEP
EARLY = 2
WIDE = 512
LOCAL_STEPS = WIDTH // WIDE
CHUNK = 2
IN_FIRST = 14
OUT_FIRST = 14
ROWS = 64
SLICE = ROWS + 8
LOG2E = math.log2(math.e)
LOG2_SCALE = -0.5 * math.log2(DK)

NT = (((1,), (1,)), ((), ()))
TN = (((0,), (0,)), ((), ()))

VMEM = pl.BlockSpec(memory_space=pltpu.VMEM)
SMEM = pl.BlockSpec(memory_space=pltpu.SMEM)
HBM = pl.BlockSpec(memory_space=pltpu.HBM)
ANY = pl.BlockSpec(memory_space=pl.ANY)


def in_vmem(x):
    return pltpu.with_memory_space_constraint(x, pltpu.VMEM)


def in_hbm(x):
    return pltpu.with_memory_space_constraint(x, pltpu.HBM)


def dot(a, b, dims=(((1,), (0,)), ((), ()))):
    return lax.dot_general(a, b, dims, preferred_element_type=jnp.float32)


def triangle(strict_upper):
    row = lax.broadcasted_iota(jnp.int32, (GROUP, 2 * GROUP), 0)
    col = lax.broadcasted_iota(jnp.int32, (GROUP, 2 * GROUP), 1)
    col = jnp.where(col >= GROUP, col - GROUP, col)
    keep = col > row if strict_upper else col <= row
    return jnp.where(keep, 1.0, 0.0).astype(jnp.bfloat16)


def partial_sums(ones, gate):
    high = gate.astype(jnp.bfloat16)
    low = (gate - high.astype(jnp.float32)).astype(jnp.bfloat16)
    return dot(ones, jnp.concatenate([high, low], axis=0))


def columns(half, step, lanes=LANES):
    return pl.ds(pl.multiple_of(half * WIDTH + step * lanes, lanes), lanes)


def states_step(step, gate_ref, key_ref, value_ref, out_ref):
    ones = triangle(True)
    state = [jnp.zeros((DV, DK), jnp.float32)] * HEADS_STEP
    total = [jnp.zeros((1, DK), jnp.float32)] * HEADS_STEP
    cols = pl.ds(step * LANES, LANES)
    for group in range(gate_ref.shape[0] // GROUP):
        rows = pl.ds(group * GROUP, GROUP)
        gate = gate_ref[rows, cols] * LOG2E
        later = partial_sums(ones, gate)
        gamma = later[0:1] + gate[0:1]
        to_end = (key_ref[rows, cols].astype(jnp.float32) * jnp.exp2(later)).astype(jnp.bfloat16)
        decay = jnp.exp2(gamma)
        for head in range(HEADS_STEP):
            at = slice(head * DK, (head + 1) * DK)
            value = value_ref[rows, pl.ds(step * LANES + head * DV, DV)]
            state[head] = state[head] * decay[:, at] + dot(value, to_end[:, at], TN)
            total[head] = total[head] + gamma[:, at]
    for head in range(HEADS_STEP):
        for part in range(2):
            at = 2 * (step * HEADS_STEP + head) + part
            out_ref[at, 0:ROWS, :] = state[head][ROWS * part : ROWS * (part + 1)]
            out_ref[at, ROWS:SLICE, :] = jnp.broadcast_to(total[head], (SLICE - ROWS, DK))


def column_copies(half, steps, sources, targets, sems, lanes=LANES):
    copies = []
    for step in steps:
        for source, target in zip(sources, targets):
            at = pl.ds(step * lanes, lanes)
            copies.append(
                pltpu.make_async_copy(source.at[:, columns(half, step, lanes)], target.at[:, at], sems.at[len(copies)])
            )
    return [copies[i : i + len(sources)] for i in range(0, len(copies), len(sources))]


def start_all(copies):
    for copy in copies:
        copy.start()


def wait_all(copies):
    for copy in copies:
        copy.wait()


def rest_states_kernel(
    core_ref, gate_hbm, key_hbm, value_hbm, out_ref, own_gate, own_key, own_value, gate, key, value, sems, own_sems
):
    sources = (gate_hbm, key_hbm, value_hbm)
    mine = column_copies(1 - core_ref[0], range(STEPS), sources, (gate, key, value), sems)
    early = column_copies(core_ref[0], range(EARLY), sources, (own_gate, own_key, own_value), own_sems)
    for copies in mine:
        start_all(copies)
    for step in range(STEPS):
        wait_all(mine[step])
        if step == 0:
            for copies in early:
                start_all(copies)
        states_step(step, gate, key, value, out_ref)
    for copies in early:
        wait_all(copies)


def rest_states(core, gate, keys, values):
    tokens = keys.shape[0]
    kinds = [x.dtype for x in (gate, keys, values)]
    return pl.pallas_call(
        rest_states_kernel,
        in_specs=[SMEM, HBM, HBM, HBM],
        out_specs=[VMEM] * 4,
        out_shape=[pltpu.VMEM((2 * HALF, SLICE, DK), jnp.float32)]
        + [pltpu.VMEM((tokens, EARLY * LANES), kind) for kind in kinds],
        scratch_shapes=[pltpu.VMEM((tokens, WIDTH), kind) for kind in kinds]
        + [pltpu.SemaphoreType.DMA((3 * STEPS,)), pltpu.SemaphoreType.DMA((3 * EARLY,))],
        compiler_params=pltpu.CompilerParams(vmem_limit_bytes=8 << 20),
        cost_estimate=pl.CostEstimate(flops=10**9, bytes_accessed=9 * 10**6, transcendentals=10**6),
        name="rest_states",
    )(core, in_hbm(gate), in_hbm(keys), in_hbm(values))


def own_states_kernel(
    core_ref, gate_hbm, key_hbm, value_hbm, early_gate, early_key, early_value, out_ref, gate, key, value, sems
):
    mine = column_copies(
        core_ref[0], range(EARLY, STEPS), (gate_hbm, key_hbm, value_hbm), (gate, key, value), sems
    )
    for copies in mine:
        start_all(copies)
    for step in range(EARLY):
        states_step(step, early_gate, early_key, early_value, out_ref)
    for step in range(EARLY, STEPS):
        wait_all(mine[step - EARLY])
        states_step(step, gate, key, value, out_ref)


def own_states(core, gate, keys, values, early):
    tokens = keys.shape[0]
    kinds = [x.dtype for x in (gate, keys, values)]
    return pl.pallas_call(
        own_states_kernel,
        in_specs=[SMEM, HBM, HBM, HBM] + [VMEM] * 3,
        out_specs=VMEM,
        out_shape=pltpu.VMEM((2 * HALF, SLICE, DK), jnp.float32),
        scratch_shapes=[pltpu.VMEM((tokens, WIDTH), kind) for kind in kinds]
        + [pltpu.SemaphoreType.DMA((3 * (STEPS - EARLY),))],
        compiler_params=pltpu.CompilerParams(vmem_limit_bytes=8 << 20),
        cost_estimate=pl.CostEstimate(flops=10**9, bytes_accessed=5 * 10**6, transcendentals=10**6),
        name="own_states",
    )(core, in_hbm(gate), in_hbm(keys), in_hbm(values), *map(in_vmem, early))


def combine_kernel(core_ref, mine_ref, other_ref, out_ref, keep_ref):
    first = core_ref[0] == 0
    mine_total = mine_ref[:, ROWS:SLICE, :]
    other_total = other_ref[:, ROWS:SLICE, :]
    mine_weight = jnp.where(first, jnp.exp2(other_total), 1.0)[:, 0:1]
    other_weight = jnp.where(first, 1.0, jnp.exp2(mine_total))[:, 0:1]
    mine = mine_ref[:, 0:ROWS, :]
    other = other_ref[:, 0:ROWS, :]
    out_ref[:, 0:ROWS, :] = mine * mine_weight + other * other_weight
    out_ref[:, ROWS:SLICE, :] = mine_total + other_total
    keep_ref[:, 0:ROWS, :] = jnp.where(first, mine, other)
    keep_ref[:, ROWS:SLICE, :] = jnp.where(first, mine_total, other_total)


def combine(core, mine, other):
    return pl.pallas_call(
        combine_kernel,
        in_specs=[SMEM, VMEM, VMEM],
        out_specs=[VMEM, VMEM],
        out_shape=[pltpu.VMEM(mine.shape, jnp.float32)] * 2,
        compiler_params=pltpu.CompilerParams(vmem_limit_bytes=4 << 20),
        name="combine",
    )(core, in_vmem(mine), in_vmem(other))


def advance_kernel(core_ref, entry_ref, keep_ref, mine_ref, sent_ref):
    first = core_ref[0] == 0
    chips = entry_ref.shape[0]
    for at in range(chips):
        entry = entry_ref[(at + IN_FIRST - OUT_FIRST) % chips]
        advanced = entry * jnp.exp2(keep_ref[at, ROWS : ROWS + 1, :]) + keep_ref[at, 0:ROWS, :]
        mine_ref[at] = jnp.where(first, entry, advanced)
        sent_ref[at] = jnp.where(first, advanced, entry)


def advance(core, entry, keep):
    return pl.pallas_call(
        advance_kernel,
        in_specs=[SMEM, VMEM, VMEM],
        out_specs=[VMEM, VMEM],
        out_shape=[pltpu.VMEM(entry.shape, jnp.float32)] * 2,
        compiler_params=pltpu.CompilerParams(vmem_limit_bytes=4 << 20),
        name="advance",
    )(core, in_vmem(entry), in_vmem(keep))


def prefix_kernel(in_ref, out_hbm, done_ref, out_ref, sems):
    done_ref[...] = jnp.zeros_like(done_ref)
    running = jnp.zeros((ROWS, DK), jnp.float32)
    chips = in_ref.shape[0]
    copies = []
    for chip in range(chips):
        out_ref[(chip - OUT_FIRST) % chips] = running
        if chip % CHUNK == CHUNK - 1:
            at = pl.ds((chip + 1 - CHUNK - OUT_FIRST) % chips, CHUNK)
            copies.append(pltpu.make_async_copy(out_ref.at[at], out_hbm.at[at], sems.at[len(copies)]))
            copies[-1].start()
        if chip < chips - 1:
            place = (chip - IN_FIRST) % chips
            decay = jnp.exp2(in_ref[place, ROWS : ROWS + 1, :])
            running = running * decay + in_ref[place, 0:ROWS, :]
    wait_all(copies)


def prefix(received):
    shape = (received.shape[0], ROWS, DK)
    return pl.pallas_call(
        prefix_kernel,
        in_specs=[VMEM],
        out_specs=[HBM, VMEM],
        out_shape=[pltpu.HBM(shape, jnp.float32), jax.ShapeDtypeStruct((8, DK), jnp.float32)],
        scratch_shapes=[pltpu.VMEM(shape, jnp.float32), pltpu.SemaphoreType.DMA((shape[0] // CHUNK,))],
        compiler_params=pltpu.CompilerParams(vmem_limit_bytes=4 << 20),
        name="prefix",
    )(in_vmem(received))


def local_step(step, waits, query_ref, key_ref, value_ref, gate_ref, local_ref, decayed_ref, stored):
    ones = triangle(False)
    row = lax.broadcasted_iota(jnp.int32, (GROUP, GROUP), 0)
    col = lax.broadcasted_iota(jnp.int32, (GROUP, GROUP), 1)
    causal = row >= col
    cols = pl.ds(step * WIDE, WIDE)
    groups = range(gate_ref.shape[0] // GROUP)
    heads = range(WIDE // DK)
    rows = [pl.ds(group * GROUP, GROUP) for group in groups]
    at = [slice(head * DK, (head + 1) * DK) for head in heads]
    waits[0]()
    sums = [partial_sums(ones, gate_ref[rows[group], cols] * LOG2E) for group in groups]
    gamma = [inclusive[GROUP - 1 : GROUP] for inclusive in sums]
    decay = [jnp.exp2(total) for total in gamma]
    waits[1]()
    queries, keys, to_end = [], [], []
    before = None
    for group in groups:
        query = query_ref[rows[group], cols].astype(jnp.float32) * jnp.exp2(sums[group] + LOG2_SCALE)
        key = key_ref[rows[group], cols].astype(jnp.float32) * jnp.exp2(-sums[group])
        queries.append(query.astype(jnp.bfloat16))
        keys.append(key.astype(jnp.bfloat16))
        to_end.append((key * decay[group]).astype(jnp.bfloat16))
        if group == 0:
            decayed_ref[rows[group], cols] = queries[group]
            before = gamma[group]
        else:
            decayed_ref[rows[group], cols] = (query * jnp.exp2(before)).astype(jnp.bfloat16)
            before = before + gamma[group]
    stored(0, cols)
    value_cols = [pl.ds(step * WIDE + head * DV, DV) for head in heads]
    scores = [[dot(queries[group][:, at[head]], keys[group][:, at[head]], NT) for head in heads] for group in groups]
    scores = [[jnp.where(causal, x, 0.0).astype(jnp.bfloat16) for x in line] for line in scores]
    updates = [
        [dot(value_ref[rows[group], value_cols[head]], to_end[group][:, at[head]], TN) for head in heads]
        for group in groups[:-1]
    ]
    for head in heads:
        state = None
        for group in groups:
            value = value_ref[rows[group], value_cols[head]]
            if group == 0:
                out = dot(scores[group][head], value)
                state = updates[group][head]
            else:
                left = jnp.concatenate([scores[group][head], queries[group][:, at[head]]], axis=1)
                out = dot(left, jnp.concatenate([value, state.astype(jnp.bfloat16).T], axis=0))
                if group < groups[-1]:
                    state = state * decay[group][:, at[head]] + updates[group][head]
            local_ref[rows[group], value_cols[head]] = out.astype(local_ref.dtype)
    stored(1, cols)


def local_kernel(*refs):
    core_ref, query_hbm, key_hbm, value_hbm, gate_hbm, _ = refs[:6]
    own_local, own_decayed, rest_local_hbm, rest_decayed_hbm, done_ref = refs[6:11]
    query, key, value, gate, rest_local, rest_decayed, first, sems, first_sem, store_sems = refs[11:]
    core = core_ref[0]
    steps = range(LOCAL_STEPS)
    queue = []
    for i, half in ((0, 1 - core), (1, core)):
        targets = tuple(x.at[i] for x in (gate, key, query, value))
        queue += column_copies(half, steps, (gate_hbm, key_hbm, query_hbm, value_hbm), targets, sems.at[i], WIDE)
    early = pltpu.make_async_copy(gate_hbm.at[0:8, 0:DK], first, first_sem)
    early.start()
    start_all(queue[0])
    early.wait()
    start_all(queue[1])
    stores = []

    def store(which, cols):
        ref, out = ((rest_decayed, rest_decayed_hbm), (rest_local, rest_local_hbm))[which]
        stores.append(pltpu.make_async_copy(ref.at[:, cols], out.at[:, cols], store_sems.at[len(stores)]))
        stores[-1].start()

    for i, out, decayed, stored in (
        (0, rest_local, rest_decayed, store),
        (1, own_local, own_decayed, lambda which, cols: None),
    ):
        inputs = [x.at[i] for x in (query, key, value, gate)]
        for step in steps:
            place = i * LOCAL_STEPS + step

            def gates(place=place):
                queue[place][0].wait()
                if place + 2 < len(queue):
                    start_all(queue[place + 2])

            local_step(step, (gates, lambda place=place: wait_all(queue[place][1:])), *inputs, out, decayed, stored)
    done_ref[...] = jnp.zeros_like(done_ref)
    wait_all(stores)


def local_part(core, queries, keys, values, gate, after):
    tokens = keys.shape[0]
    half = ((tokens, WIDTH), jnp.bfloat16)
    return pl.pallas_call(
        local_kernel,
        in_specs=[SMEM] + [HBM] * 4 + [ANY],
        out_specs=[VMEM, VMEM, HBM, HBM, VMEM],
        out_shape=[pltpu.VMEM(*half)] * 2 + [pltpu.HBM(*half)] * 2 + [jax.ShapeDtypeStruct((8, DK), jnp.float32)],
        scratch_shapes=[pltpu.VMEM((2, tokens, WIDTH), x.dtype) for x in (queries, keys, values, gate)]
        + [pltpu.VMEM(*half)] * 2
        + [pltpu.VMEM((8, DK), jnp.float32), pltpu.SemaphoreType.DMA((2, 4 * LOCAL_STEPS))]
        + [pltpu.SemaphoreType.DMA, pltpu.SemaphoreType.DMA((2 * LOCAL_STEPS,))],
        compiler_params=pltpu.CompilerParams(vmem_limit_bytes=32 << 20),
        cost_estimate=pl.CostEstimate(flops=8 * 10**9, bytes_accessed=16 * 10**6, transcendentals=10**6),
        name="local_part",
    )(core, in_hbm(queries), in_hbm(keys), in_hbm(values), in_hbm(gate), after)


def final_step(step, local_ref, decayed_ref, entry_ref, out_ref):
    for head in range(step * HEADS_STEP, (step + 1) * HEADS_STEP):
        at = slice(head * DK, (head + 1) * DK)
        across = dot(decayed_ref[:, at], entry_ref[at, :].astype(jnp.bfloat16), NT)
        out_ref[:, at] = (local_ref[:, at].astype(jnp.float32) + across).astype(jnp.bfloat16)


def final_steps(half, local_ref, decayed_ref, entry_ref, out_hbm, out_ref, sems):
    copies = []
    for step in range(STEPS):
        final_step(step, local_ref, decayed_ref, entry_ref, out_ref)
        at = pl.ds(step * LANES, LANES)
        copies.append(pltpu.make_async_copy(out_ref.at[:, at], out_hbm.at[:, columns(half, step)], sems.at[step]))
        copies[-1].start()
    wait_all(copies)


def own_final_kernel(core_ref, local, decayed, entry, local_hbm, decayed_hbm, _, out_hbm, rest_local, rest_decayed, *refs):
    out_ref, sems, fetch_sems = refs
    fetches = [
        pltpu.make_async_copy(local_hbm, rest_local, fetch_sems.at[0]),
        pltpu.make_async_copy(decayed_hbm, rest_decayed, fetch_sems.at[1]),
    ]
    for fetch in fetches:
        fetch.start()
    final_steps(core_ref[0], local, decayed, entry, out_hbm, out_ref, sems)
    wait_all(fetches)


def own_final(core, local, decayed, entry, rest_local, rest_decayed, after):
    tokens = local.shape[0]
    return pl.pallas_call(
        own_final_kernel,
        in_specs=[SMEM] + [VMEM] * 3 + [HBM] * 2 + [ANY],
        out_specs=[HBM, VMEM, VMEM],
        out_shape=[jax.ShapeDtypeStruct((tokens, H * DV), jnp.bfloat16)]
        + [pltpu.VMEM(x.shape, x.dtype) for x in (rest_local, rest_decayed)],
        scratch_shapes=[
            pltpu.VMEM((tokens, WIDTH), jnp.bfloat16),
            pltpu.SemaphoreType.DMA((STEPS,)),
            pltpu.SemaphoreType.DMA((2,)),
        ],
        compiler_params=pltpu.CompilerParams(vmem_limit_bytes=8 << 20),
        cost_estimate=pl.CostEstimate(flops=10**9, bytes_accessed=4 * 10**6, transcendentals=0),
        name="own_final",
    )(core, *map(in_vmem, (local, decayed, entry)), in_hbm(rest_local), in_hbm(rest_decayed), after)


def rest_final_kernel(core_ref, local, decayed, entry, _, out_hbm, out_ref, sems):
    final_steps(1 - core_ref[0], local, decayed, entry, out_hbm, out_ref, sems)


def rest_final(core, local, decayed, entry, out):
    tokens = local.shape[0]
    return pl.pallas_call(
        rest_final_kernel,
        in_specs=[SMEM] + [VMEM] * 3 + [ANY],
        out_specs=HBM,
        out_shape=jax.ShapeDtypeStruct((tokens, H * DV), jnp.bfloat16),
        input_output_aliases={4: 0},
        scratch_shapes=[pltpu.VMEM((tokens, WIDTH), jnp.bfloat16), pltpu.SemaphoreType.DMA((STEPS,))],
        compiler_params=pltpu.CompilerParams(vmem_limit_bytes=8 << 20),
        cost_estimate=pl.CostEstimate(flops=10**9, bytes_accessed=4 * 10**6, transcendentals=0),
        name="rest_final",
    )(core, *map(in_vmem, (local, decayed, entry)), out)


def on_device(queries, keys, values, log_gate):
    devices = lax.axis_size("seq")
    chips = devices // 2
    core = lax.rem(lax.axis_index("seq"), 2).astype(jnp.int32)[None]
    swap = [(i, i ^ 1) for i in range(devices)]

    def exchange(blocks, first):
        same_core = [[2 * ((place + first) % chips) + c for place in range(chips)] for c in range(2)]
        return lax.all_to_all(blocks, "seq", split_axis=0, concat_axis=0, axis_index_groups=same_core, tiled=True)

    rest, *early = rest_states(core, log_gate, keys, values)
    own_other = lax.ppermute(rest, "seq", swap)
    own = own_states(core, log_gate, keys, values, early)
    combined, keep = combine(core, own, own_other)
    entries, after = prefix(exchange(combined, IN_FIRST))
    entry = exchange(entries, OUT_FIRST)
    own_local, own_decayed, rest_local, rest_decayed, after = local_part(core, queries, keys, values, log_gate, after)
    entry, after = lax.optimization_barrier((entry, after))
    own_entry, sent = advance(core, entry, keep)
    rest_entry = lax.ppermute(sent, "seq", swap).reshape(HALF * DV, DK)
    own_entry = own_entry.reshape(HALF * DV, DK)
    out, local, decayed = own_final(core, own_local, own_decayed, own_entry, rest_local, rest_decayed, after)
    return rest_final(core, local, decayed, rest_entry, out)


def solution(mesh):
    spec = P(("batch", "seq"), None)
    return jax.shard_map(on_device, mesh=mesh, in_specs=(spec,) * 4, out_specs=spec, check_vma=False)
```

```python
import functools
import math

import jax
import jax.numpy as jnp
from jax import lax
from jax.experimental import pallas as pl
from jax.experimental.pallas import tpu as pltpu
from jax.sharding import PartitionSpec as P

H = 16
DK = 128
DV = 128
GROUP = 128
HALF = H // 2
WIDTH = HALF * DK
HEADS_STEP = 2
LANES = HEADS_STEP * DK
STEPS = HALF // HEADS_STEP
EARLY = 2
WIDE = 512
LOCAL_STEPS = WIDTH // WIDE
CHUNK = 2
FIRST = (14, 6)
ROWS = 64
SLICE = ROWS + 8
LOG2E = math.log2(math.e)
LOG2_SCALE = -0.5 * math.log2(DK)

NT = (((1,), (1,)), ((), ()))
TN = (((0,), (0,)), ((), ()))

VMEM = pl.BlockSpec(memory_space=pltpu.VMEM)
SMEM = pl.BlockSpec(memory_space=pltpu.SMEM)
HBM = pl.BlockSpec(memory_space=pltpu.HBM)
ANY = pl.BlockSpec(memory_space=pl.ANY)


def in_vmem(x):
    return pltpu.with_memory_space_constraint(x, pltpu.VMEM)


def in_hbm(x):
    return pltpu.with_memory_space_constraint(x, pltpu.HBM)


def dot(a, b, dims=(((1,), (0,)), ((), ()))):
    return lax.dot_general(a, b, dims, preferred_element_type=jnp.float32)


def triangle(strict_upper):
    row = lax.broadcasted_iota(jnp.int32, (GROUP, 2 * GROUP), 0)
    col = lax.broadcasted_iota(jnp.int32, (GROUP, 2 * GROUP), 1)
    col = jnp.where(col >= GROUP, col - GROUP, col)
    keep = col > row if strict_upper else col <= row
    return jnp.where(keep, 1.0, 0.0).astype(jnp.bfloat16)


def partial_sums(ones, gate):
    high = gate.astype(jnp.bfloat16)
    low = (gate - high.astype(jnp.float32)).astype(jnp.bfloat16)
    return dot(ones, jnp.concatenate([high, low], axis=0))


def columns(half, step, lanes=LANES):
    return pl.ds(pl.multiple_of(half * WIDTH + step * lanes, lanes), lanes)


def states_step(step, gate_ref, key_ref, value_ref, out_ref):
    ones = triangle(True)
    state = [jnp.zeros((DV, DK), jnp.float32)] * HEADS_STEP
    total = [jnp.zeros((1, DK), jnp.float32)] * HEADS_STEP
    cols = pl.ds(step * LANES, LANES)
    for group in range(gate_ref.shape[0] // GROUP):
        rows = pl.ds(group * GROUP, GROUP)
        gate = gate_ref[rows, cols] * LOG2E
        later = partial_sums(ones, gate)
        gamma = later[0:1] + gate[0:1]
        to_end = (key_ref[rows, cols].astype(jnp.float32) * jnp.exp2(later)).astype(jnp.bfloat16)
        decay = jnp.exp2(gamma)
        for head in range(HEADS_STEP):
            at = slice(head * DK, (head + 1) * DK)
            value = value_ref[rows, pl.ds(step * LANES + head * DV, DV)]
            state[head] = state[head] * decay[:, at] + dot(value, to_end[:, at], TN)
            total[head] = total[head] + gamma[:, at]
    for head in range(HEADS_STEP):
        for part in range(2):
            at = 2 * (step * HEADS_STEP + head) + part
            out_ref[at, 0:ROWS, :] = state[head][ROWS * part : ROWS * (part + 1)]
            out_ref[at, ROWS:SLICE, :] = jnp.broadcast_to(total[head], (SLICE - ROWS, DK))


def column_copies(half, steps, sources, targets, sems, lanes=LANES):
    copies = []
    for step in steps:
        for source, target in zip(sources, targets):
            at = pl.ds(step * lanes, lanes)
            copies.append(
                pltpu.make_async_copy(source.at[:, columns(half, step, lanes)], target.at[:, at], sems.at[len(copies)])
            )
    return [copies[i : i + len(sources)] for i in range(0, len(copies), len(sources))]


def start_all(copies):
    for copy in copies:
        copy.start()


def wait_all(copies):
    for copy in copies:
        copy.wait()


def rest_states_kernel(
    core_ref, gate_hbm, key_hbm, value_hbm, out_ref, own_gate, own_key, own_value, gate, key, value, sems, own_sems
):
    sources = (gate_hbm, key_hbm, value_hbm)
    mine = column_copies(1 - core_ref[0], range(STEPS), sources, (gate, key, value), sems)
    early = column_copies(core_ref[0], range(EARLY), sources, (own_gate, own_key, own_value), own_sems)
    for copies in mine:
        start_all(copies)
    for step in range(STEPS):
        wait_all(mine[step])
        if step == 0:
            for copies in early:
                start_all(copies)
        states_step(step, gate, key, value, out_ref)
    for copies in early:
        wait_all(copies)


def rest_states(core, gate, keys, values):
    tokens = keys.shape[0]
    kinds = [x.dtype for x in (gate, keys, values)]
    return pl.pallas_call(
        rest_states_kernel,
        in_specs=[SMEM, HBM, HBM, HBM],
        out_specs=[VMEM] * 4,
        out_shape=[pltpu.VMEM((2 * HALF, SLICE, DK), jnp.float32)]
        + [pltpu.VMEM((tokens, EARLY * LANES), kind) for kind in kinds],
        scratch_shapes=[pltpu.VMEM((tokens, WIDTH), kind) for kind in kinds]
        + [pltpu.SemaphoreType.DMA((3 * STEPS,)), pltpu.SemaphoreType.DMA((3 * EARLY,))],
        compiler_params=pltpu.CompilerParams(vmem_limit_bytes=8 << 20),
        cost_estimate=pl.CostEstimate(flops=10**9, bytes_accessed=9 * 10**6, transcendentals=10**6),
        name="rest_states",
    )(core, in_hbm(gate), in_hbm(keys), in_hbm(values))


def own_states_kernel(
    core_ref, gate_hbm, key_hbm, value_hbm, early_gate, early_key, early_value, out_ref, gate, key, value, sems
):
    mine = column_copies(
        core_ref[0], range(EARLY, STEPS), (gate_hbm, key_hbm, value_hbm), (gate, key, value), sems
    )
    for copies in mine:
        start_all(copies)
    for step in range(EARLY):
        states_step(step, early_gate, early_key, early_value, out_ref)
    for step in range(EARLY, STEPS):
        wait_all(mine[step - EARLY])
        states_step(step, gate, key, value, out_ref)


def own_states(core, gate, keys, values, early):
    tokens = keys.shape[0]
    kinds = [x.dtype for x in (gate, keys, values)]
    return pl.pallas_call(
        own_states_kernel,
        in_specs=[SMEM, HBM, HBM, HBM] + [VMEM] * 3,
        out_specs=VMEM,
        out_shape=pltpu.VMEM((2 * HALF, SLICE, DK), jnp.float32),
        scratch_shapes=[pltpu.VMEM((tokens, WIDTH), kind) for kind in kinds]
        + [pltpu.SemaphoreType.DMA((3 * (STEPS - EARLY),))],
        compiler_params=pltpu.CompilerParams(vmem_limit_bytes=8 << 20),
        cost_estimate=pl.CostEstimate(flops=10**9, bytes_accessed=5 * 10**6, transcendentals=10**6),
        name="own_states",
    )(core, in_hbm(gate), in_hbm(keys), in_hbm(values), *map(in_vmem, early))


def combine_kernel(core_ref, mine_ref, other_ref, out_ref, keep_ref):
    first = core_ref[0] == 0
    mine_total = mine_ref[:, ROWS:SLICE, :]
    other_total = other_ref[:, ROWS:SLICE, :]
    mine_weight = jnp.where(first, jnp.exp2(other_total), 1.0)[:, 0:1]
    other_weight = jnp.where(first, 1.0, jnp.exp2(mine_total))[:, 0:1]
    mine = mine_ref[:, 0:ROWS, :]
    other = other_ref[:, 0:ROWS, :]
    out_ref[:, 0:ROWS, :] = mine * mine_weight + other * other_weight
    out_ref[:, ROWS:SLICE, :] = mine_total + other_total
    keep_ref[:, 0:ROWS, :] = jnp.where(first, mine, other)
    keep_ref[:, ROWS:SLICE, :] = jnp.where(first, mine_total, other_total)


def combine(core, mine, other):
    return pl.pallas_call(
        combine_kernel,
        in_specs=[SMEM, VMEM, VMEM],
        out_specs=[VMEM, VMEM],
        out_shape=[pltpu.VMEM(mine.shape, jnp.float32)] * 2,
        compiler_params=pltpu.CompilerParams(vmem_limit_bytes=4 << 20),
        name="combine",
    )(core, in_vmem(mine), in_vmem(other))


def advance_kernel(core_ref, entry_ref, keep_ref, mine_ref, sent_ref):
    first = core_ref[0] == 0
    for at in range(entry_ref.shape[0]):
        entry = entry_ref[at]
        advanced = entry * jnp.exp2(keep_ref[at, ROWS : ROWS + 1, :]) + keep_ref[at, 0:ROWS, :]
        mine_ref[at] = jnp.where(first, entry, advanced)
        sent_ref[at] = jnp.where(first, advanced, entry)


def advance(core, entry, keep):
    return pl.pallas_call(
        advance_kernel,
        in_specs=[SMEM, VMEM, VMEM],
        out_specs=[VMEM, VMEM],
        out_shape=[pltpu.VMEM(entry.shape, jnp.float32)] * 2,
        compiler_params=pltpu.CompilerParams(vmem_limit_bytes=4 << 20),
        name="advance",
    )(core, in_vmem(entry), in_vmem(keep))


def prefix_kernel(core_ref, in_ref, out_hbm, done_ref, out_ref, sems):
    done_ref[...] = jnp.zeros_like(done_ref)
    running = jnp.zeros((ROWS, DK), jnp.float32)
    chips = in_ref.shape[0]
    shift = jnp.where(core_ref[0] == 0, chips - FIRST[0], chips - FIRST[1])
    copies = []
    for chip in range(chips):
        place = lax.rem(chip + shift, chips)
        out_ref[place] = running
        if chip % CHUNK == CHUNK - 1:
            at = pl.ds(place + 1 - CHUNK, CHUNK)
            copies.append(pltpu.make_async_copy(out_ref.at[at], out_hbm.at[at], sems.at[len(copies)]))
            copies[-1].start()
        if chip < chips - 1:
            decay = jnp.exp2(in_ref[place, ROWS : ROWS + 1, :])
            running = running * decay + in_ref[place, 0:ROWS, :]
    wait_all(copies)


def prefix(core, received):
    shape = (received.shape[0], ROWS, DK)
    return pl.pallas_call(
        prefix_kernel,
        in_specs=[SMEM, VMEM],
        out_specs=[HBM, VMEM],
        out_shape=[pltpu.HBM(shape, jnp.float32), jax.ShapeDtypeStruct((8, DK), jnp.float32)],
        scratch_shapes=[pltpu.VMEM(shape, jnp.float32), pltpu.SemaphoreType.DMA((shape[0] // CHUNK,))],
        compiler_params=pltpu.CompilerParams(vmem_limit_bytes=4 << 20),
        name="prefix",
    )(core, in_vmem(received))


def local_step(step, waits, query_ref, key_ref, value_ref, gate_ref, local_ref, decayed_ref, stored):
    ones = triangle(False)
    row = lax.broadcasted_iota(jnp.int32, (GROUP, GROUP), 0)
    col = lax.broadcasted_iota(jnp.int32, (GROUP, GROUP), 1)
    causal = row >= col
    cols = pl.ds(step * WIDE, WIDE)
    groups = range(gate_ref.shape[0] // GROUP)
    heads = range(WIDE // DK)
    rows = [pl.ds(group * GROUP, GROUP) for group in groups]
    at = [slice(head * DK, (head + 1) * DK) for head in heads]
    waits[0]()
    sums = [partial_sums(ones, gate_ref[rows[group], cols] * LOG2E) for group in groups]
    gamma = [inclusive[GROUP - 1 : GROUP] for inclusive in sums]
    decay = [jnp.exp2(total) for total in gamma]
    waits[1]()
    queries, keys, to_end = [], [], []
    before = None
    for group in groups:
        query = query_ref[rows[group], cols].astype(jnp.float32) * jnp.exp2(sums[group] + LOG2_SCALE)
        key = key_ref[rows[group], cols].astype(jnp.float32) * jnp.exp2(-sums[group])
        queries.append(query.astype(jnp.bfloat16))
        keys.append(key.astype(jnp.bfloat16))
        to_end.append((key * decay[group]).astype(jnp.bfloat16))
        if group == 0:
            decayed_ref[rows[group], cols] = queries[group]
            before = gamma[group]
        else:
            decayed_ref[rows[group], cols] = (query * jnp.exp2(before)).astype(jnp.bfloat16)
            before = before + gamma[group]
    stored(0, cols)
    value_cols = [pl.ds(step * WIDE + head * DV, DV) for head in heads]
    scores = [[dot(queries[group][:, at[head]], keys[group][:, at[head]], NT) for head in heads] for group in groups]
    scores = [[jnp.where(causal, x, 0.0).astype(jnp.bfloat16) for x in line] for line in scores]
    updates = [
        [dot(value_ref[rows[group], value_cols[head]], to_end[group][:, at[head]], TN) for head in heads]
        for group in groups[:-1]
    ]
    for head in heads:
        state = None
        for group in groups:
            value = value_ref[rows[group], value_cols[head]]
            if group == 0:
                out = dot(scores[group][head], value)
                state = updates[group][head]
            else:
                left = jnp.concatenate([scores[group][head], queries[group][:, at[head]]], axis=1)
                out = dot(left, jnp.concatenate([value, state.astype(jnp.bfloat16).T], axis=0))
                if group < groups[-1]:
                    state = state * decay[group][:, at[head]] + updates[group][head]
            local_ref[rows[group], value_cols[head]] = out.astype(local_ref.dtype)
    stored(1, cols)


def local_kernel(*refs):
    core_ref, query_hbm, key_hbm, value_hbm, gate_hbm, _ = refs[:6]
    own_local, own_decayed, rest_local_hbm, rest_decayed_hbm, done_ref = refs[6:11]
    query, key, value, gate, rest_local, rest_decayed, first, sems, first_sem, store_sems = refs[11:]
    core = core_ref[0]
    steps = range(LOCAL_STEPS)
    queue = []
    for i, half in ((0, 1 - core), (1, core)):
        targets = tuple(x.at[i] for x in (gate, key, query, value))
        queue += column_copies(half, steps, (gate_hbm, key_hbm, query_hbm, value_hbm), targets, sems.at[i], WIDE)
    early = pltpu.make_async_copy(gate_hbm.at[0:8, 0:DK], first, first_sem)
    early.start()
    start_all(queue[0])
    early.wait()
    start_all(queue[1])
    stores = []

    def store(which, cols):
        ref, out = ((rest_decayed, rest_decayed_hbm), (rest_local, rest_local_hbm))[which]
        stores.append(pltpu.make_async_copy(ref.at[:, cols], out.at[:, cols], store_sems.at[len(stores)]))
        stores[-1].start()

    for i, out, decayed, stored in (
        (0, rest_local, rest_decayed, store),
        (1, own_local, own_decayed, lambda which, cols: None),
    ):
        inputs = [x.at[i] for x in (query, key, value, gate)]
        for step in steps:
            place = i * LOCAL_STEPS + step

            def gates(place=place):
                queue[place][0].wait()
                if place + 2 < len(queue):
                    start_all(queue[place + 2])

            local_step(step, (gates, lambda place=place: wait_all(queue[place][1:])), *inputs, out, decayed, stored)
    done_ref[...] = jnp.zeros_like(done_ref)
    wait_all(stores)


def local_part(core, queries, keys, values, gate, after):
    tokens = keys.shape[0]
    half = ((tokens, WIDTH), jnp.bfloat16)
    return pl.pallas_call(
        local_kernel,
        in_specs=[SMEM] + [HBM] * 4 + [ANY],
        out_specs=[VMEM, VMEM, HBM, HBM, VMEM],
        out_shape=[pltpu.VMEM(*half)] * 2 + [pltpu.HBM(*half)] * 2 + [jax.ShapeDtypeStruct((8, DK), jnp.float32)],
        scratch_shapes=[pltpu.VMEM((2, tokens, WIDTH), x.dtype) for x in (queries, keys, values, gate)]
        + [pltpu.VMEM(*half)] * 2
        + [pltpu.VMEM((8, DK), jnp.float32), pltpu.SemaphoreType.DMA((2, 4 * LOCAL_STEPS))]
        + [pltpu.SemaphoreType.DMA, pltpu.SemaphoreType.DMA((2 * LOCAL_STEPS,))],
        compiler_params=pltpu.CompilerParams(vmem_limit_bytes=32 << 20),
        cost_estimate=pl.CostEstimate(flops=8 * 10**9, bytes_accessed=16 * 10**6, transcendentals=10**6),
        name="local_part",
    )(core, in_hbm(queries), in_hbm(keys), in_hbm(values), in_hbm(gate), after)


def final_step(step, local_ref, decayed_ref, entry_ref, out_ref):
    for head in range(step * HEADS_STEP, (step + 1) * HEADS_STEP):
        at = slice(head * DK, (head + 1) * DK)
        across = dot(decayed_ref[:, at], entry_ref[at, :].astype(jnp.bfloat16), NT)
        out_ref[:, at] = (local_ref[:, at].astype(jnp.float32) + across).astype(jnp.bfloat16)


def final_steps(half, local_ref, decayed_ref, entry_ref, out_hbm, out_ref, sems):
    copies = []
    for step in range(STEPS):
        final_step(step, local_ref, decayed_ref, entry_ref, out_ref)
        at = pl.ds(step * LANES, LANES)
        copies.append(pltpu.make_async_copy(out_ref.at[:, at], out_hbm.at[:, columns(half, step)], sems.at[step]))
        copies[-1].start()
    wait_all(copies)


def own_final_kernel(core_ref, local, decayed, entry, local_hbm, decayed_hbm, _, out_hbm, rest_local, rest_decayed, *refs):
    out_ref, sems, fetch_sems = refs
    fetches = [
        pltpu.make_async_copy(local_hbm, rest_local, fetch_sems.at[0]),
        pltpu.make_async_copy(decayed_hbm, rest_decayed, fetch_sems.at[1]),
    ]
    for fetch in fetches:
        fetch.start()
    final_steps(core_ref[0], local, decayed, entry, out_hbm, out_ref, sems)
    wait_all(fetches)


def own_final(core, local, decayed, entry, rest_local, rest_decayed, after):
    tokens = local.shape[0]
    return pl.pallas_call(
        own_final_kernel,
        in_specs=[SMEM] + [VMEM] * 3 + [HBM] * 2 + [ANY],
        out_specs=[HBM, VMEM, VMEM],
        out_shape=[jax.ShapeDtypeStruct((tokens, H * DV), jnp.bfloat16)]
        + [pltpu.VMEM(x.shape, x.dtype) for x in (rest_local, rest_decayed)],
        scratch_shapes=[
            pltpu.VMEM((tokens, WIDTH), jnp.bfloat16),
            pltpu.SemaphoreType.DMA((STEPS,)),
            pltpu.SemaphoreType.DMA((2,)),
        ],
        compiler_params=pltpu.CompilerParams(vmem_limit_bytes=8 << 20),
        cost_estimate=pl.CostEstimate(flops=10**9, bytes_accessed=4 * 10**6, transcendentals=0),
        name="own_final",
    )(core, *map(in_vmem, (local, decayed, entry)), in_hbm(rest_local), in_hbm(rest_decayed), after)


def rest_final_kernel(core_ref, local, decayed, entry, _, out_hbm, out_ref, sems):
    final_steps(1 - core_ref[0], local, decayed, entry, out_hbm, out_ref, sems)


def rest_final(core, local, decayed, entry, out):
    tokens = local.shape[0]
    return pl.pallas_call(
        rest_final_kernel,
        in_specs=[SMEM] + [VMEM] * 3 + [ANY],
        out_specs=HBM,
        out_shape=jax.ShapeDtypeStruct((tokens, H * DV), jnp.bfloat16),
        input_output_aliases={4: 0},
        scratch_shapes=[pltpu.VMEM((tokens, WIDTH), jnp.bfloat16), pltpu.SemaphoreType.DMA((STEPS,))],
        compiler_params=pltpu.CompilerParams(vmem_limit_bytes=8 << 20),
        cost_estimate=pl.CostEstimate(flops=10**9, bytes_accessed=4 * 10**6, transcendentals=0),
        name="rest_final",
    )(core, *map(in_vmem, (local, decayed, entry)), out)


def on_device(queries, keys, values, log_gate):
    devices = lax.axis_size("seq")
    chips = devices // 2
    core = lax.rem(lax.axis_index("seq"), 2).astype(jnp.int32)[None]
    swap = [(i, i ^ 1) for i in range(devices)]

    def exchange(blocks):
        same_core = [[2 * ((place + FIRST[c]) % chips) + c for place in range(chips)] for c in range(2)]
        return lax.all_to_all(blocks, "seq", split_axis=0, concat_axis=0, axis_index_groups=same_core, tiled=True)

    rest, *early = rest_states(core, log_gate, keys, values)
    own_other = lax.ppermute(rest, "seq", swap)
    own = own_states(core, log_gate, keys, values, early)
    combined, keep = combine(core, own, own_other)
    entries, after = prefix(core, exchange(combined))
    entry = exchange(entries)
    own_local, own_decayed, rest_local, rest_decayed, after = local_part(core, queries, keys, values, log_gate, after)
    entry, after = lax.optimization_barrier((entry, after))
    own_entry, sent = advance(core, entry, keep)
    rest_entry = lax.ppermute(sent, "seq", swap).reshape(HALF * DV, DK)
    own_entry = own_entry.reshape(HALF * DV, DK)
    out, local, decayed = own_final(core, own_local, own_decayed, own_entry, rest_local, rest_decayed, after)
    return rest_final(core, local, decayed, rest_entry, out)


def solution(mesh):
    spec = P(("batch", "seq"), None)
    return jax.shard_map(on_device, mesh=mesh, in_specs=(spec,) * 4, out_specs=spec, check_vma=False)
```

```python
import functools
import math

import jax
import jax.numpy as jnp
from jax import lax
from jax.experimental import pallas as pl
from jax.experimental.pallas import tpu as pltpu
from jax.sharding import PartitionSpec as P

H = 16
DK = 128
DV = 128
GROUP = 128
HALF = H // 2
WIDTH = HALF * DK
HEADS_STEP = 2
LANES = HEADS_STEP * DK
STEPS = HALF // HEADS_STEP
EARLY = 2
WIDE = 512
LOCAL_STEPS = WIDTH // WIDE
CHUNK = 2
FIRST = (10, 6)
ROWS = 64
SLICE = ROWS + 8
LOG2E = math.log2(math.e)
LOG2_SCALE = -0.5 * math.log2(DK)

NT = (((1,), (1,)), ((), ()))
TN = (((0,), (0,)), ((), ()))

VMEM = pl.BlockSpec(memory_space=pltpu.VMEM)
SMEM = pl.BlockSpec(memory_space=pltpu.SMEM)
HBM = pl.BlockSpec(memory_space=pltpu.HBM)
ANY = pl.BlockSpec(memory_space=pl.ANY)


def in_vmem(x):
    return pltpu.with_memory_space_constraint(x, pltpu.VMEM)


def in_hbm(x):
    return pltpu.with_memory_space_constraint(x, pltpu.HBM)


def dot(a, b, dims=(((1,), (0,)), ((), ()))):
    return lax.dot_general(a, b, dims, preferred_element_type=jnp.float32)


def triangle(strict_upper):
    row = lax.broadcasted_iota(jnp.int32, (GROUP, 2 * GROUP), 0)
    col = lax.broadcasted_iota(jnp.int32, (GROUP, 2 * GROUP), 1)
    col = jnp.where(col >= GROUP, col - GROUP, col)
    keep = col > row if strict_upper else col <= row
    return jnp.where(keep, 1.0, 0.0).astype(jnp.bfloat16)


def partial_sums(ones, gate):
    high = gate.astype(jnp.bfloat16)
    low = (gate - high.astype(jnp.float32)).astype(jnp.bfloat16)
    return dot(ones, jnp.concatenate([high, low], axis=0))


def columns(half, step, lanes=LANES):
    return pl.ds(pl.multiple_of(half * WIDTH + step * lanes, lanes), lanes)


def states_step(step, gate_ref, key_ref, value_ref, out_ref):
    ones = triangle(True)
    state = [jnp.zeros((DV, DK), jnp.float32)] * HEADS_STEP
    total = [jnp.zeros((1, DK), jnp.float32)] * HEADS_STEP
    cols = pl.ds(step * LANES, LANES)
    for group in range(gate_ref.shape[0] // GROUP):
        rows = pl.ds(group * GROUP, GROUP)
        gate = gate_ref[rows, cols] * LOG2E
        later = partial_sums(ones, gate)
        gamma = later[0:1] + gate[0:1]
        to_end = (key_ref[rows, cols].astype(jnp.float32) * jnp.exp2(later)).astype(jnp.bfloat16)
        decay = jnp.exp2(gamma)
        for head in range(HEADS_STEP):
            at = slice(head * DK, (head + 1) * DK)
            value = value_ref[rows, pl.ds(step * LANES + head * DV, DV)]
            state[head] = state[head] * decay[:, at] + dot(value, to_end[:, at], TN)
            total[head] = total[head] + gamma[:, at]
    for head in range(HEADS_STEP):
        for part in range(2):
            at = 2 * (step * HEADS_STEP + head) + part
            out_ref[at, 0:ROWS, :] = state[head][ROWS * part : ROWS * (part + 1)]
            out_ref[at, ROWS:SLICE, :] = jnp.broadcast_to(total[head], (SLICE - ROWS, DK))


def column_copies(half, steps, sources, targets, sems, lanes=LANES):
    copies = []
    for step in steps:
        for source, target in zip(sources, targets):
            at = pl.ds(step * lanes, lanes)
            copies.append(
                pltpu.make_async_copy(source.at[:, columns(half, step, lanes)], target.at[:, at], sems.at[len(copies)])
            )
    return [copies[i : i + len(sources)] for i in range(0, len(copies), len(sources))]


def start_all(copies):
    for copy in copies:
        copy.start()


def wait_all(copies):
    for copy in copies:
        copy.wait()


def rest_states_kernel(
    core_ref, gate_hbm, key_hbm, value_hbm, out_ref, own_gate, own_key, own_value, gate, key, value, sems, own_sems
):
    sources = (gate_hbm, key_hbm, value_hbm)
    mine = column_copies(1 - core_ref[0], range(STEPS), sources, (gate, key, value), sems)
    early = column_copies(core_ref[0], range(EARLY), sources, (own_gate, own_key, own_value), own_sems)
    for copies in mine:
        start_all(copies)
    for step in range(STEPS):
        wait_all(mine[step])
        if step == 0:
            for copies in early:
                start_all(copies)
        states_step(step, gate, key, value, out_ref)
    for copies in early:
        wait_all(copies)


def rest_states(core, gate, keys, values):
    tokens = keys.shape[0]
    kinds = [x.dtype for x in (gate, keys, values)]
    return pl.pallas_call(
        rest_states_kernel,
        in_specs=[SMEM, HBM, HBM, HBM],
        out_specs=[VMEM] * 4,
        out_shape=[pltpu.VMEM((2 * HALF, SLICE, DK), jnp.float32)]
        + [pltpu.VMEM((tokens, EARLY * LANES), kind) for kind in kinds],
        scratch_shapes=[pltpu.VMEM((tokens, WIDTH), kind) for kind in kinds]
        + [pltpu.SemaphoreType.DMA((3 * STEPS,)), pltpu.SemaphoreType.DMA((3 * EARLY,))],
        compiler_params=pltpu.CompilerParams(vmem_limit_bytes=8 << 20),
        cost_estimate=pl.CostEstimate(flops=10**9, bytes_accessed=9 * 10**6, transcendentals=10**6),
        name="rest_states",
    )(core, in_hbm(gate), in_hbm(keys), in_hbm(values))


def own_states_kernel(
    core_ref, gate_hbm, key_hbm, value_hbm, early_gate, early_key, early_value, out_ref, gate, key, value, sems
):
    mine = column_copies(
        core_ref[0], range(EARLY, STEPS), (gate_hbm, key_hbm, value_hbm), (gate, key, value), sems
    )
    for copies in mine:
        start_all(copies)
    for step in range(EARLY):
        states_step(step, early_gate, early_key, early_value, out_ref)
    for step in range(EARLY, STEPS):
        wait_all(mine[step - EARLY])
        states_step(step, gate, key, value, out_ref)


def own_states(core, gate, keys, values, early):
    tokens = keys.shape[0]
    kinds = [x.dtype for x in (gate, keys, values)]
    return pl.pallas_call(
        own_states_kernel,
        in_specs=[SMEM, HBM, HBM, HBM] + [VMEM] * 3,
        out_specs=VMEM,
        out_shape=pltpu.VMEM((2 * HALF, SLICE, DK), jnp.float32),
        scratch_shapes=[pltpu.VMEM((tokens, WIDTH), kind) for kind in kinds]
        + [pltpu.SemaphoreType.DMA((3 * (STEPS - EARLY),))],
        compiler_params=pltpu.CompilerParams(vmem_limit_bytes=8 << 20),
        cost_estimate=pl.CostEstimate(flops=10**9, bytes_accessed=5 * 10**6, transcendentals=10**6),
        name="own_states",
    )(core, in_hbm(gate), in_hbm(keys), in_hbm(values), *map(in_vmem, early))


def combine_kernel(core_ref, mine_ref, other_ref, out_ref, keep_ref):
    first = core_ref[0] == 0
    mine_total = mine_ref[:, ROWS:SLICE, :]
    other_total = other_ref[:, ROWS:SLICE, :]
    mine_weight = jnp.where(first, jnp.exp2(other_total), 1.0)[:, 0:1]
    other_weight = jnp.where(first, 1.0, jnp.exp2(mine_total))[:, 0:1]
    mine = mine_ref[:, 0:ROWS, :]
    other = other_ref[:, 0:ROWS, :]
    out_ref[:, 0:ROWS, :] = mine * mine_weight + other * other_weight
    out_ref[:, ROWS:SLICE, :] = mine_total + other_total
    keep_ref[:, 0:ROWS, :] = jnp.where(first, mine, other)
    keep_ref[:, ROWS:SLICE, :] = jnp.where(first, mine_total, other_total)


def combine(core, mine, other):
    return pl.pallas_call(
        combine_kernel,
        in_specs=[SMEM, VMEM, VMEM],
        out_specs=[VMEM, VMEM],
        out_shape=[pltpu.VMEM(mine.shape, jnp.float32)] * 2,
        compiler_params=pltpu.CompilerParams(vmem_limit_bytes=4 << 20),
        name="combine",
    )(core, in_vmem(mine), in_vmem(other))


def advance_kernel(core_ref, entry_ref, keep_ref, mine_ref, sent_ref):
    first = core_ref[0] == 0
    for at in range(entry_ref.shape[0]):
        entry = entry_ref[at]
        advanced = entry * jnp.exp2(keep_ref[at, ROWS : ROWS + 1, :]) + keep_ref[at, 0:ROWS, :]
        mine_ref[at] = jnp.where(first, entry, advanced)
        sent_ref[at] = jnp.where(first, advanced, entry)


def advance(core, entry, keep):
    return pl.pallas_call(
        advance_kernel,
        in_specs=[SMEM, VMEM, VMEM],
        out_specs=[VMEM, VMEM],
        out_shape=[pltpu.VMEM(entry.shape, jnp.float32)] * 2,
        compiler_params=pltpu.CompilerParams(vmem_limit_bytes=4 << 20),
        name="advance",
    )(core, in_vmem(entry), in_vmem(keep))


def prefix_kernel(core_ref, in_ref, out_hbm, done_ref, out_ref, sems):
    done_ref[...] = jnp.zeros_like(done_ref)
    running = jnp.zeros((ROWS, DK), jnp.float32)
    chips = in_ref.shape[0]
    shift = jnp.where(core_ref[0] == 0, chips - FIRST[0], chips - FIRST[1])
    copies = []
    for chip in range(chips):
        place = lax.rem(chip + shift, chips)
        out_ref[place] = running
        if chip % CHUNK == CHUNK - 1:
            at = pl.ds(place + 1 - CHUNK, CHUNK)
            copies.append(pltpu.make_async_copy(out_ref.at[at], out_hbm.at[at], sems.at[len(copies)]))
            copies[-1].start()
        if chip < chips - 1:
            decay = jnp.exp2(in_ref[place, ROWS : ROWS + 1, :])
            running = running * decay + in_ref[place, 0:ROWS, :]
    wait_all(copies)


def prefix(core, received):
    shape = (received.shape[0], ROWS, DK)
    return pl.pallas_call(
        prefix_kernel,
        in_specs=[SMEM, VMEM],
        out_specs=[HBM, VMEM],
        out_shape=[pltpu.HBM(shape, jnp.float32), jax.ShapeDtypeStruct((8, DK), jnp.float32)],
        scratch_shapes=[pltpu.VMEM(shape, jnp.float32), pltpu.SemaphoreType.DMA((shape[0] // CHUNK,))],
        compiler_params=pltpu.CompilerParams(vmem_limit_bytes=4 << 20),
        name="prefix",
    )(core, in_vmem(received))


def local_step(step, waits, query_ref, key_ref, value_ref, gate_ref, local_ref, decayed_ref, stored):
    ones = triangle(False)
    row = lax.broadcasted_iota(jnp.int32, (GROUP, GROUP), 0)
    col = lax.broadcasted_iota(jnp.int32, (GROUP, GROUP), 1)
    causal = row >= col
    cols = pl.ds(step * WIDE, WIDE)
    groups = range(gate_ref.shape[0] // GROUP)
    heads = range(WIDE // DK)
    rows = [pl.ds(group * GROUP, GROUP) for group in groups]
    at = [slice(head * DK, (head + 1) * DK) for head in heads]
    waits[0]()
    sums = [partial_sums(ones, gate_ref[rows[group], cols] * LOG2E) for group in groups]
    gamma = [inclusive[GROUP - 1 : GROUP] for inclusive in sums]
    decay = [jnp.exp2(total) for total in gamma]
    waits[1]()
    queries, keys, to_end = [], [], []
    before = None
    for group in groups:
        query = query_ref[rows[group], cols].astype(jnp.float32) * jnp.exp2(sums[group] + LOG2_SCALE)
        key = key_ref[rows[group], cols].astype(jnp.float32) * jnp.exp2(-sums[group])
        queries.append(query.astype(jnp.bfloat16))
        keys.append(key.astype(jnp.bfloat16))
        to_end.append((key * decay[group]).astype(jnp.bfloat16))
        if group == 0:
            decayed_ref[rows[group], cols] = queries[group]
            before = gamma[group]
        else:
            decayed_ref[rows[group], cols] = (query * jnp.exp2(before)).astype(jnp.bfloat16)
            before = before + gamma[group]
    stored(0, cols)
    value_cols = [pl.ds(step * WIDE + head * DV, DV) for head in heads]
    scores = [[dot(queries[group][:, at[head]], keys[group][:, at[head]], NT) for head in heads] for group in groups]
    scores = [[jnp.where(causal, x, 0.0).astype(jnp.bfloat16) for x in line] for line in scores]
    updates = [
        [dot(value_ref[rows[group], value_cols[head]], to_end[group][:, at[head]], TN) for head in heads]
        for group in groups[:-1]
    ]
    for head in heads:
        state = None
        for group in groups:
            value = value_ref[rows[group], value_cols[head]]
            if group == 0:
                out = dot(scores[group][head], value)
                state = updates[group][head]
            else:
                left = jnp.concatenate([scores[group][head], queries[group][:, at[head]]], axis=1)
                out = dot(left, jnp.concatenate([value, state.astype(jnp.bfloat16).T], axis=0))
                if group < groups[-1]:
                    state = state * decay[group][:, at[head]] + updates[group][head]
            local_ref[rows[group], value_cols[head]] = out.astype(local_ref.dtype)
    stored(1, cols)


def local_kernel(*refs):
    core_ref, query_hbm, key_hbm, value_hbm, gate_hbm, _ = refs[:6]
    own_local, own_decayed, rest_local_hbm, rest_decayed_hbm, done_ref = refs[6:11]
    query, key, value, gate, rest_local, rest_decayed, first, sems, first_sem, store_sems = refs[11:]
    core = core_ref[0]
    steps = range(LOCAL_STEPS)
    queue = []
    for i, half in ((0, 1 - core), (1, core)):
        targets = tuple(x.at[i] for x in (gate, key, query, value))
        queue += column_copies(half, steps, (gate_hbm, key_hbm, query_hbm, value_hbm), targets, sems.at[i], WIDE)
    early = pltpu.make_async_copy(gate_hbm.at[0:8, 0:DK], first, first_sem)
    early.start()
    start_all(queue[0])
    early.wait()
    start_all(queue[1])
    stores = []

    def store(which, cols):
        ref, out = ((rest_decayed, rest_decayed_hbm), (rest_local, rest_local_hbm))[which]
        stores.append(pltpu.make_async_copy(ref.at[:, cols], out.at[:, cols], store_sems.at[len(stores)]))
        stores[-1].start()

    for i, out, decayed, stored in (
        (0, rest_local, rest_decayed, store),
        (1, own_local, own_decayed, lambda which, cols: None),
    ):
        inputs = [x.at[i] for x in (query, key, value, gate)]
        for step in steps:
            place = i * LOCAL_STEPS + step

            def gates(place=place):
                queue[place][0].wait()
                if place + 2 < len(queue):
                    start_all(queue[place + 2])

            local_step(step, (gates, lambda place=place: wait_all(queue[place][1:])), *inputs, out, decayed, stored)
    done_ref[...] = jnp.zeros_like(done_ref)
    wait_all(stores)


def local_part(core, queries, keys, values, gate, after):
    tokens = keys.shape[0]
    half = ((tokens, WIDTH), jnp.bfloat16)
    return pl.pallas_call(
        local_kernel,
        in_specs=[SMEM] + [HBM] * 4 + [ANY],
        out_specs=[VMEM, VMEM, HBM, HBM, VMEM],
        out_shape=[pltpu.VMEM(*half)] * 2 + [pltpu.HBM(*half)] * 2 + [jax.ShapeDtypeStruct((8, DK), jnp.float32)],
        scratch_shapes=[pltpu.VMEM((2, tokens, WIDTH), x.dtype) for x in (queries, keys, values, gate)]
        + [pltpu.VMEM(*half)] * 2
        + [pltpu.VMEM((8, DK), jnp.float32), pltpu.SemaphoreType.DMA((2, 4 * LOCAL_STEPS))]
        + [pltpu.SemaphoreType.DMA, pltpu.SemaphoreType.DMA((2 * LOCAL_STEPS,))],
        compiler_params=pltpu.CompilerParams(vmem_limit_bytes=32 << 20),
        cost_estimate=pl.CostEstimate(flops=8 * 10**9, bytes_accessed=16 * 10**6, transcendentals=10**6),
        name="local_part",
    )(core, in_hbm(queries), in_hbm(keys), in_hbm(values), in_hbm(gate), after)


def final_step(step, local_ref, decayed_ref, entry_ref, out_ref):
    for head in range(step * HEADS_STEP, (step + 1) * HEADS_STEP):
        at = slice(head * DK, (head + 1) * DK)
        across = dot(decayed_ref[:, at], entry_ref[at, :].astype(jnp.bfloat16), NT)
        out_ref[:, at] = (local_ref[:, at].astype(jnp.float32) + across).astype(jnp.bfloat16)


def final_steps(half, local_ref, decayed_ref, entry_ref, out_hbm, out_ref, sems):
    copies = []
    for step in range(STEPS):
        final_step(step, local_ref, decayed_ref, entry_ref, out_ref)
        at = pl.ds(step * LANES, LANES)
        copies.append(pltpu.make_async_copy(out_ref.at[:, at], out_hbm.at[:, columns(half, step)], sems.at[step]))
        copies[-1].start()
    wait_all(copies)


def own_final_kernel(core_ref, local, decayed, entry, local_hbm, decayed_hbm, _, out_hbm, rest_local, rest_decayed, *refs):
    out_ref, sems, fetch_sems = refs
    fetches = [
        pltpu.make_async_copy(local_hbm, rest_local, fetch_sems.at[0]),
        pltpu.make_async_copy(decayed_hbm, rest_decayed, fetch_sems.at[1]),
    ]
    for fetch in fetches:
        fetch.start()
    final_steps(core_ref[0], local, decayed, entry, out_hbm, out_ref, sems)
    wait_all(fetches)


def own_final(core, local, decayed, entry, rest_local, rest_decayed, after):
    tokens = local.shape[0]
    return pl.pallas_call(
        own_final_kernel,
        in_specs=[SMEM] + [VMEM] * 3 + [HBM] * 2 + [ANY],
        out_specs=[HBM, VMEM, VMEM],
        out_shape=[jax.ShapeDtypeStruct((tokens, H * DV), jnp.bfloat16)]
        + [pltpu.VMEM(x.shape, x.dtype) for x in (rest_local, rest_decayed)],
        scratch_shapes=[
            pltpu.VMEM((tokens, WIDTH), jnp.bfloat16),
            pltpu.SemaphoreType.DMA((STEPS,)),
            pltpu.SemaphoreType.DMA((2,)),
        ],
        compiler_params=pltpu.CompilerParams(vmem_limit_bytes=8 << 20),
        cost_estimate=pl.CostEstimate(flops=10**9, bytes_accessed=4 * 10**6, transcendentals=0),
        name="own_final",
    )(core, *map(in_vmem, (local, decayed, entry)), in_hbm(rest_local), in_hbm(rest_decayed), after)


def rest_final_kernel(core_ref, local, decayed, entry, _, out_hbm, out_ref, sems):
    final_steps(1 - core_ref[0], local, decayed, entry, out_hbm, out_ref, sems)


def rest_final(core, local, decayed, entry, out):
    tokens = local.shape[0]
    return pl.pallas_call(
        rest_final_kernel,
        in_specs=[SMEM] + [VMEM] * 3 + [ANY],
        out_specs=HBM,
        out_shape=jax.ShapeDtypeStruct((tokens, H * DV), jnp.bfloat16),
        input_output_aliases={4: 0},
        scratch_shapes=[pltpu.VMEM((tokens, WIDTH), jnp.bfloat16), pltpu.SemaphoreType.DMA((STEPS,))],
        compiler_params=pltpu.CompilerParams(vmem_limit_bytes=8 << 20),
        cost_estimate=pl.CostEstimate(flops=10**9, bytes_accessed=4 * 10**6, transcendentals=0),
        name="rest_final",
    )(core, *map(in_vmem, (local, decayed, entry)), out)


def on_device(queries, keys, values, log_gate):
    devices = lax.axis_size("seq")
    chips = devices // 2
    core = lax.rem(lax.axis_index("seq"), 2).astype(jnp.int32)[None]
    swap = [(i, i ^ 1) for i in range(devices)]

    def exchange(blocks):
        same_core = [[2 * ((place + FIRST[c]) % chips) + c for place in range(chips)] for c in range(2)]
        return lax.all_to_all(blocks, "seq", split_axis=0, concat_axis=0, axis_index_groups=same_core, tiled=True)

    rest, *early = rest_states(core, log_gate, keys, values)
    own_other = lax.ppermute(rest, "seq", swap)
    own = own_states(core, log_gate, keys, values, early)
    combined, keep = combine(core, own, own_other)
    entries, after = prefix(core, exchange(combined))
    entry = exchange(entries)
    own_local, own_decayed, rest_local, rest_decayed, after = local_part(core, queries, keys, values, log_gate, after)
    entry, after = lax.optimization_barrier((entry, after))
    own_entry, sent = advance(core, entry, keep)
    rest_entry = lax.ppermute(sent, "seq", swap).reshape(HALF * DV, DK)
    own_entry = own_entry.reshape(HALF * DV, DK)
    out, local, decayed = own_final(core, own_local, own_decayed, own_entry, rest_local, rest_decayed, after)
    return rest_final(core, local, decayed, rest_entry, out)


def solution(mesh):
    spec = P(("batch", "seq"), None)
    return jax.shard_map(on_device, mesh=mesh, in_specs=(spec,) * 4, out_specs=spec, check_vma=False)
```
